512 devices in a mesh: rowa: 16 (over z), rowb: 32 (over y, x, core).
Axes of the slice: x: 4, y: 4, z: 16, core: 2. Of those that a mesh axis runs over, the one named last changes fastest.
Arguments:
- slab: bfloat16 [262144, 1024], P(('rowa', 'rowb')), may hold values from -6 to 6, as said below
- panel: bfloat16 [64, 262144], P(None, ('rowa', 'rowb')), may hold values from -6 to 6
Outputs:
- basis_out: float32 [64, 262144], P(None, ('rowa', 'rowb'))
- factor_out: float32 [64, 64], replicated
The draws below stay inside these ranges and needn't reach their ends.
Inputs may be any that keep to these rules, and one draw needn't show every extreme that they name: Real valued entries of the slab.
All inputs are finite; a program needn't handle non-finite values.
Results may differ from the reference program's by a relative error of at most 0.0055.
Values may be sent and summed in bfloat16 or wider, within the bound.
A program may use at most 64 MiB of HBM per device.

```python
import math
import jax
import jax.numpy as jnp
from jax import lax

D = 1024
K = 64
ITERS = 3
ROWS = 262144


def draw_slab(key, part):
    key = jax.random.fold_in(key, 11)
    key_noise, key_col, key_row = jax.random.split(key, 3)
    noise = jnp.clip(jax.random.normal(key_noise, (ROWS, D), jnp.float32), -4.0, 4.0)
    top = 3.0
    climb = 8.0
    column = jnp.exp(jax.random.uniform(key_col, (1, D), jnp.float32) * math.log(top))
    column = column / math.sqrt((top * top - 1.0) / (2.0 * math.log(top)))
    rowscale = jnp.exp(jax.random.uniform(key_row, (ROWS, 1), jnp.float32) * math.log(10.0))
    rowscale = rowscale / math.sqrt(99.0 / (2.0 * math.log(10.0)))
    position = jnp.arange(ROWS, dtype=jnp.float32).reshape(ROWS, 1) / float(ROWS)
    rising = jnp.exp(position * math.log(climb))
    rising = rising / math.sqrt((climb * climb - 1.0) / (2.0 * math.log(climb)))
    return (noise * column * rowscale * rising * D ** (-0.25)).astype(jnp.bfloat16)


def block_scale(stream_key, extent, cuts, smallest, high):
    level, own = 1.0, jax.random.fold_in(stream_key, 6)
    for dim, shards_of in cuts:
        draws = jnp.exp(jax.random.uniform(jax.random.fold_in(own, dim), (shards_of,), jnp.float32, smallest / len(cuts), high / len(cuts)))
        level = level * jnp.repeat(draws, extent[dim] // shards_of).reshape([-1 if axis == dim else 1 for axis in range(len(extent))])
    return level


def gaussian(stream_key, extent, deviation, limit, pieces=(), kind=jnp.bfloat16):
    loudness = block_scale(stream_key, extent, pieces, -0.22, 0.18) if pieces else 1.0
    values = jax.random.normal(stream_key, extent, jnp.float32) * deviation * loudness
    return jnp.minimum(jnp.maximum(values, -limit), limit).astype(kind)


def setup_inputs(seed: int = 0) -> dict:
    splits = jax.random.split(jax.random.key(seed), 3)
    return {
        "slab": draw_slab(jax.random.fold_in(splits[2], 71), 0),
        "panel": gaussian(splits[1], (K, ROWS), 1.0, 6.0, ((1, 512),)),
    }


def reference(slab, panel):
    current = panel
    basis = None
    lower = None
    for step in range(ITERS):
        projected = jnp.dot(current.astype(jnp.float32), slab.astype(jnp.float32), preferred_element_type=jnp.float32)
        projected_b = projected.astype(jnp.bfloat16)
        image = lax.dot_general(projected_b.astype(jnp.float32), slab.astype(jnp.float32), (((1,), (1,)), ((), ())), preferred_element_type=jnp.float32)
        gram = jnp.dot(image, image.T, precision=lax.Precision.HIGHEST)
        lower = jnp.linalg.cholesky(gram)
        basis = lax.linalg.triangular_solve(lower, image, left_side=True, lower=True)
        current = basis.astype(jnp.bfloat16)
    scale = math.sqrt(ROWS)
    return (basis * scale, lower.T / scale)
```

```python
import functools
import math

import jax
import jax.numpy as jnp
from jax import lax
from jax.experimental import pallas as pl
from jax.experimental.pallas import tpu as pltpu
from jax.sharding import PartitionSpec as P

ITERS = 3
MESH = pl.DeviceIdType.MESH
F32 = jnp.float32
BF16 = jnp.bfloat16
LANE = 128
CORES = 2
PANEL = 4


def dot(a, b):
    return jnp.dot(a, b, preferred_element_type=F32)


def dot_t(a, b):
    return lax.dot_general(a, b, (((1,), (1,)), ((), ())), preferred_element_type=F32)


def split(v):
    high = v.astype(BF16)
    return high, (v - high.astype(F32)).astype(BF16)


def factor_rows(m, k):
    groups = [m[8 * i : 8 * i + 8, :] for i in range(k // 8)]
    full = groups[0].shape
    done = [[None] * 8 for _ in groups]
    for first in range(0, k, PANEL):
        g, s = divmod(first, 8)
        size = range(PANEL)
        rows = [jnp.broadcast_to(groups[g][s + q : s + q + 1, :], full) for q in size]
        cols = [
            {i: jnp.broadcast_to(groups[i][:, first + q : first + q + 1], full) for i in range(g, len(groups))}
            for q in size
        ]
        piv = [[jnp.broadcast_to(cols[r][g][s + q : s + q + 1, :], full) for r in size] for q in size]
        inv = []
        for q in size:
            inv.append(1.0 / piv[q][q])
            for r in range(q + 1, PANEL):
                t = piv[q][r] * inv[q]
                rows[r] = rows[r] - t * rows[q]
                for i in cols[r]:
                    cols[r][i] = cols[r][i] - t * cols[q][i]
                for w in range(r, PANEL):
                    piv[r][w] = piv[r][w] - t * piv[q][w]
            done[g][s + q] = rows[q] * lax.rsqrt(piv[q][q])
        for i in range(g, len(groups)):
            new = groups[i]
            for q in size:
                new = new - (cols[q][i] * inv[q]) * rows[q]
            groups[i] = new
    sub = lax.broadcasted_iota(jnp.int32, full, 0)
    out = []
    for rows in done:
        v = rows[0]
        for q in range(1, 8):
            v = jnp.where(sub == q, rows[q], v)
        out.append(v)
    return jnp.concatenate(out, axis=0)


def kernel(dims, tiles, scale, slab_ref, panel_ref, basis_ref, factor_ref,
           part, got_c, acc, got_1, mid, got_2, own, got_z, total, g_high, g_low, w_high, w_low, p_pad, sems):
    nz, ny, nx = dims
    k, d = panel_ref.shape[0], slab_ref.shape[1]
    nb = d // LANE
    half = part.shape[0] // CORES
    stream = half // 2
    rows_1 = (stream // nx, stream // ny)
    rows_2 = stream // (nx * ny)
    tile = 2 * rows_2 // tiles

    z = lax.axis_index("rowa")
    b = lax.axis_index("rowb")
    c = lax.rem(b, CORES)
    x = lax.rem(b // CORES, nx)
    y = b // (CORES * nx)

    def device(zz, yy, xx, cc):
        return (zz, (yy * nx + xx) * CORES + cc)

    other = device(z, y, x, 1 - c)
    peers_x = [device(z, y, lax.rem(x + q, nx), c) for q in range(1, nx)]
    peers_y = [device(z, lax.rem(y + q, ny), x, c) for q in range(1, ny)]
    peers_z = [device(lax.rem(z + q, nz), y, x, c) for q in range(1, nz)]

    barrier = pltpu.get_barrier_semaphore()
    everyone = [other] + peers_x + peers_y + peers_z
    for peer in everyone:
        pl.semaphore_signal(barrier, inc=1, device_id=peer, device_id_type=MESH)

    used = [0]

    def new_sems(n):
        at = used[0]
        used[0] += n
        return at

    def copy(src, dst, send, recv, peer):
        return pltpu.make_async_remote_copy(
            src_ref=src, dst_ref=dst, send_sem=sems.at[send], recv_sem=sems.at[recv], device_id=peer, device_id_type=MESH
        )

    at = 0
    for i in range(nb):
        left = slab_ref[:, i * LANE : (i + 1) * LANE].T
        g = dot(left, slab_ref[:, i * LANE :])
        for j in range(i, nb):
            part[at * LANE : (at + 1) * LANE, :] = g[:, (j - i) * LANE : (j - i + 1) * LANE]
            at += 1
    first = dot(panel_ref[...], slab_ref[...])
    for j in range(nb):
        part[at * LANE + j * k : at * LANE + (j + 1) * k, :] = first[:, j * LANE : (j + 1) * LANE]

    pl.semaphore_wait(barrier, len(everyone))

    sent = []
    s, r = new_sems(1), new_sems(1)
    cp = copy(part.at[pl.ds(pl.multiple_of((1 - c) * half, half), half)], got_c, s, r, other)
    cp.start()
    cp.wait_recv()
    sent.append(cp)
    acc[...] = part[pl.ds(pl.multiple_of(c * half, half), half), :] + got_c[...]

    streams = ((nx, x, peers_x, ny, y, peers_y), (ny, y, peers_y, nx, x, peers_x))
    waits = []
    for i, (n1, me1, peers1, _, _, _) in enumerate(streams):
        s, r = new_sems(n1 - 1), new_sems(n1 - 1)
        for q in range(1, n1):
            to = lax.rem(me1 + q, n1)
            src = acc.at[pl.ds(pl.multiple_of(i * stream + to * rows_1[i], 16), rows_1[i])]
            cp = copy(src, got_1.at[i, q - 1], s + q - 1, r + q - 1, peers1[q - 1])
            cp.start()
            waits.append(cp)
    for i, (n1, me1, _, _, _, _) in enumerate(streams):
        for cp in waits[i * (n1 - 1) : (i + 1) * (n1 - 1)]:
            cp.wait_recv()
        v = acc[pl.ds(pl.multiple_of(i * stream + me1 * rows_1[i], 16), rows_1[i]), :]
        for q in range(n1 - 1):
            v = v + got_1[i, q]
        mid[i] = v
    sent += waits

    waits = []
    for i, (_, _, _, n2, me2, peers2) in enumerate(streams):
        s, r = new_sems(n2 - 1), new_sems(n2 - 1)
        for q in range(1, n2):
            to = lax.rem(me2 + q, n2)
            src = mid.at[i, pl.ds(pl.multiple_of(to * rows_2, 16), rows_2)]
            cp = copy(src, got_2.at[i, q - 1], s + q - 1, r + q - 1, peers2[q - 1])
            cp.start()
            waits.append(cp)
    for i, (_, _, _, n2, me2, _) in enumerate(streams):
        for cp in waits[i * (n2 - 1) : (i + 1) * (n2 - 1)]:
            cp.wait_recv()
        v = mid[i, pl.ds(pl.multiple_of(me2 * rows_2, 16), rows_2), :]
        for q in range(n2 - 1):
            v = v + got_2[i, q]
        own[i * rows_2 : (i + 1) * rows_2, :] = v
    sent += waits

    owners = [(t * nz) // tiles for t in range(tiles)]
    bases = [c * half + x * rows_1[0] + y * rows_2, c * half + stream + y * rows_1[1] + x * rows_2]
    mine = (z * tiles + nz - 1) // nz
    is_owner = (mine * nz) // tiles == z
    half_tiles = tiles // 2
    s_z, r_z = new_sems(tiles), new_sems(nz - 1)

    def to_owner(t):
        slot = lax.rem(z - owners[t] + nz - 1 + nz, nz)
        return copy(own.at[pl.ds(t * tile, tile)], got_z.at[slot], s_z + t, r_z + slot, device(owners[t], y, x, c))

    for t in range(tiles):
        @pl.when(z != owners[t])
        def _():
            to_owner(t).start()

    def tile_rows(t, hi_half):
        base = jnp.where(hi_half, bases[1] + (t - half_tiles) * tile, bases[0] + t * tile)
        return pl.ds(pl.multiple_of(base, 16), tile)

    s_g, r_g = new_sems(nz - 1), new_sems(tiles)

    @pl.when(is_owner)
    def _():
        v = own[pl.ds(pl.multiple_of(mine * tile, 16), tile), :]
        for q in range(nz - 1):
            copy(own.at[pl.ds(0, tile)], got_z.at[q], s_z, r_z + q, other).wait_recv()
        for q in range(nz - 1):
            v = v + got_z[q]
        where = tile_rows(mine, mine >= half_tiles)
        total[where, :] = v
        for q in range(nz - 1):
            copy(total.at[where], total.at[where], s_g + q, r_g + mine, peers_z[q]).start()

    for t in range(tiles):
        i = t // half_tiles
        where = pl.ds(pl.multiple_of(bases[i] + (t - i * half_tiles) * tile, 16), tile)

        @pl.when(z != owners[t])
        def _():
            copy(total.at[where], total.at[where], s_g, r_g + t, other).wait_recv()

    waits = []
    for i, (_, _, _, n2, me2, peers2) in enumerate(streams):
        s, r = new_sems(n2 - 1), new_sems(n2 - 1)
        where = total.at[pl.ds(pl.multiple_of(bases[i], 16), rows_2)]
        for q in range(1, n2):
            cp = copy(where, where, s + q - 1, r + q - 1, peers2[q - 1])
            cp.start()
            waits.append(cp)
    for cp in waits:
        cp.wait_recv()
    sent += waits

    waits = []
    for i, (n1, me1, peers1, _, _, _) in enumerate(streams):
        s, r = new_sems(n1 - 1), new_sems(n1 - 1)
        where = total.at[pl.ds(pl.multiple_of(c * half + i * stream + me1 * rows_1[i], 16), rows_1[i])]
        for q in range(1, n1):
            cp = copy(where, where, s + q - 1, r + q - 1, peers1[q - 1])
            cp.start()
            waits.append(cp)
    for cp in waits:
        cp.wait_recv()
    sent += waits

    s, r = new_sems(1), new_sems(1)
    where = total.at[pl.ds(pl.multiple_of(c * half, half), half)]
    cp = copy(where, where, s, r, other)
    cp.start()
    cp.wait_recv()
    sent.append(cp)

    for cp in sent:
        cp.wait_send()
    for t in range(tiles):
        @pl.when(z != owners[t])
        def _():
            to_owner(t).wait_send()

    @pl.when(is_owner)
    def _():
        where = tile_rows(mine, mine >= half_tiles)
        for q in range(nz - 1):
            copy(total.at[where], total.at[where], s_g + q, r_g + mine, peers_z[q]).wait_send()

    at = 0
    for i in range(nb):
        for j in range(i, nb):
            v = total[at * LANE : (at + 1) * LANE, :]
            at += 1
            high, low = split(v)
            g_high[i * LANE : (i + 1) * LANE, j * LANE : (j + 1) * LANE] = high
            g_low[i * LANE : (i + 1) * LANE, j * LANE : (j + 1) * LANE] = low
            if j > i:
                high, low = split(v.T)
                g_high[j * LANE : (j + 1) * LANE, i * LANE : (i + 1) * LANE] = high
                g_low[j * LANE : (j + 1) * LANE, i * LANE : (i + 1) * LANE] = low

    w_high[0:k, :] = jnp.zeros((k, d), BF16)
    w_low[0:k, :] = jnp.zeros((k, d), BF16)
    p_pad[k : 2 * k, :] = jnp.zeros((k, d), BF16)
    current = jnp.concatenate(
        [total[at * LANE + j * k : at * LANE + (j + 1) * k, :] for j in range(nb)], axis=1
    )
    row = lax.broadcasted_iota(jnp.int32, (k, 2 * k), 0)
    col = lax.broadcasted_iota(jnp.int32, (k, 2 * k), 1)
    eye = jnp.where(col == row + k, 1.0, 0.0)
    for step in range(ITERS):
        pb = current.astype(BF16)
        p_pad[0:k, :] = pb
        wh, wl = split(dot(pb, g_high[...]) + dot(pb, g_low[...]))
        m = factor_rows(dot_t(wh, p_pad[...]) + dot_t(wl, p_pad[...]) + eye, k)
        mh, ml = split(m)
        if step < ITERS - 1:
            w_high[k : 2 * k, :] = wh
            w_low[k : 2 * k, :] = wl
            current = dot(mh, w_high[...]) + (dot(mh, w_low[...]) + dot(ml, w_high[...]))
        else:
            rows = slab_ref.shape[0]
            ih, il = split(dot_t(pb, slab_ref[...]))
            w_high[k : 2 * k, 0:rows] = ih
            w_low[k : 2 * k, 0:rows] = il
            ih, il = w_high[:, 0:rows], w_low[:, 0:rows]
            basis_ref[...] = (dot(mh, ih) + (dot(mh, il) + dot(ml, ih))) * scale
            factor_ref[...] = jnp.where(col >= row, m, 0.0)[:, 0:k] * (1.0 / scale)


def body(sizes, slab, panel):
    nz, ny, nx, tiles = sizes
    rows, d = slab.shape
    k = panel.shape[0]
    nb = d // LANE
    blocks = nb * (nb + 1) // 2 + nb * k // LANE
    half = blocks * LANE // CORES
    stream = half // 2
    rows_1, rows_2 = stream // nx, stream // (nx * ny)
    tile = 2 * rows_2 // tiles
    scale = math.sqrt(rows * nz * ny * nx * CORES)
    n_sems = 4 + 4 * (nx - 1 + ny - 1) * 2 + 2 * (tiles + nz - 1)
    return pl.pallas_call(
        functools.partial(kernel, (nz, ny, nx), tiles, scale),
        out_shape=(jax.ShapeDtypeStruct((k, rows), F32), jax.ShapeDtypeStruct((k, k), F32)),
        in_specs=[pl.BlockSpec(memory_space=pltpu.VMEM)] * 2,
        out_specs=(pl.BlockSpec(memory_space=pltpu.VMEM),) * 2,
        scratch_shapes=[
            pltpu.VMEM((2 * half, LANE), F32),
            pltpu.VMEM((half, LANE), F32),
            pltpu.VMEM((half, LANE), F32),
            pltpu.VMEM((2, nx - 1, rows_1, LANE), F32),
            pltpu.VMEM((2, rows_1, LANE), F32),
            pltpu.VMEM((2, ny - 1, rows_2, LANE), F32),
            pltpu.VMEM((2 * rows_2, LANE), F32),
            pltpu.VMEM((nz - 1, tile, LANE), F32),
            pltpu.VMEM((2 * half, LANE), F32),
            pltpu.VMEM((d, d), BF16),
            pltpu.VMEM((d, d), BF16),
            pltpu.VMEM((2 * k, d), BF16),
            pltpu.VMEM((2 * k, d), BF16),
            pltpu.VMEM((2 * k, d), BF16),
            pltpu.SemaphoreType.DMA((n_sems,)),
        ],
        compiler_params=pltpu.CompilerParams(
            collective_id=0, has_side_effects=True, vmem_limit_bytes=40 * 1024 * 1024
        ),
        cost_estimate=pl.CostEstimate(flops=3 * 10**9, bytes_accessed=3 * 10**6, transcendentals=0),
    )(slab, panel)


def solution(mesh):
    nz = mesh.shape["rowa"]
    side = math.isqrt(mesh.shape["rowb"] // CORES)
    tiles = 10 if nz == 16 else 2
    in_specs = (P(("rowa", "rowb"), None), P(None, ("rowa", "rowb")))
    out_specs = (P(None, ("rowa", "rowb")), P())
    return jax.shard_map(
        functools.partial(body, (nz, side, side, tiles)),
        mesh=mesh, in_specs=in_specs, out_specs=out_specs, check_vma=False,
    )
```

```python
import functools
import math

import jax
import jax.numpy as jnp
from jax import lax
from jax.experimental import pallas as pl
from jax.experimental.pallas import tpu as pltpu
from jax.sharding import PartitionSpec as P

ITERS = 3
MESH = pl.DeviceIdType.MESH
F32 = jnp.float32
BF16 = jnp.bfloat16
LANE = 128
CORES = 2
PANEL = 4


def dot(a, b):
    return jnp.dot(a, b, preferred_element_type=F32)


def dot_t(a, b):
    return lax.dot_general(a, b, (((1,), (1,)), ((), ())), preferred_element_type=F32)


def split(v):
    high = v.astype(BF16)
    return high, (v - high.astype(F32)).astype(BF16)


def factor_rows(m, k):
    groups = [m[8 * i : 8 * i + 8, :] for i in range(k // 8)]
    full = groups[0].shape
    done = [[None] * 8 for _ in groups]
    for first in range(0, k, PANEL):
        g, s = divmod(first, 8)
        size = range(PANEL)
        rows = [jnp.broadcast_to(groups[g][s + q : s + q + 1, :], full) for q in size]
        cols = [
            {i: jnp.broadcast_to(groups[i][:, first + q : first + q + 1], full) for i in range(g, len(groups))}
            for q in size
        ]
        piv = [[jnp.broadcast_to(cols[r][g][s + q : s + q + 1, :], full) for r in size] for q in size]
        inv = []
        for q in size:
            inv.append(1.0 / piv[q][q])
            for r in range(q + 1, PANEL):
                t = piv[q][r] * inv[q]
                rows[r] = rows[r] - t * rows[q]
                for i in cols[r]:
                    cols[r][i] = cols[r][i] - t * cols[q][i]
                for w in range(r, PANEL):
                    piv[r][w] = piv[r][w] - t * piv[q][w]
            done[g][s + q] = rows[q] * lax.rsqrt(piv[q][q])
        for i in range(g, len(groups)):
            new = groups[i]
            for q in size:
                new = new - (cols[q][i] * inv[q]) * rows[q]
            groups[i] = new
    sub = lax.broadcasted_iota(jnp.int32, full, 0)
    out = []
    for rows in done:
        v = rows[0]
        for q in range(1, 8):
            v = jnp.where(sub == q, rows[q], v)
        out.append(v)
    return jnp.concatenate(out, axis=0)


def reduce_kernel(dims, tiles, slab_ref, panel_ref, total,
                  part, got_c, acc, got_1, mid, got_2, own, got_z, sems):
    nz, ny, nx = dims
    k, d = panel_ref.shape[0], slab_ref.shape[1]
    nb = d // LANE
    half = part.shape[0] // CORES
    stream = half // 2
    rows_1 = (stream // nx, stream // ny)
    rows_2 = stream // (nx * ny)
    tile = 2 * rows_2 // tiles

    z = lax.axis_index("rowa")
    b = lax.axis_index("rowb")
    c = lax.rem(b, CORES)
    x = lax.rem(b // CORES, nx)
    y = b // (CORES * nx)

    def device(zz, yy, xx, cc):
        return (zz, (yy * nx + xx) * CORES + cc)

    other = device(z, y, x, 1 - c)
    peers_x = [device(z, y, lax.rem(x + q, nx), c) for q in range(1, nx)]
    peers_y = [device(z, lax.rem(y + q, ny), x, c) for q in range(1, ny)]
    peers_z = [device(lax.rem(z + q, nz), y, x, c) for q in range(1, nz)]

    barrier = pltpu.get_barrier_semaphore()
    everyone = [other] + peers_x + peers_y + peers_z
    for peer in everyone:
        pl.semaphore_signal(barrier, inc=1, device_id=peer, device_id_type=MESH)

    used = [0]

    def new_sems(n):
        at = used[0]
        used[0] += n
        return at

    def copy(src, dst, send, recv, peer):
        return pltpu.make_async_remote_copy(
            src_ref=src, dst_ref=dst, send_sem=sems.at[send], recv_sem=sems.at[recv], device_id=peer, device_id_type=MESH
        )

    at = 0
    for i in range(nb):
        left = slab_ref[:, i * LANE : (i + 1) * LANE].T
        g = dot(left, slab_ref[:, i * LANE :])
        for j in range(i, nb):
            part[at * LANE : (at + 1) * LANE, :] = g[:, (j - i) * LANE : (j - i + 1) * LANE]
            at += 1
    first = dot(panel_ref[...], slab_ref[...])
    for j in range(nb):
        part[at * LANE + j * k : at * LANE + (j + 1) * k, :] = first[:, j * LANE : (j + 1) * LANE]

    pl.semaphore_wait(barrier, len(everyone))

    sent = []
    s, r = new_sems(1), new_sems(1)
    cp = copy(part.at[pl.ds(pl.multiple_of((1 - c) * half, half), half)], got_c, s, r, other)
    cp.start()
    cp.wait_recv()
    sent.append(cp)
    acc[...] = part[pl.ds(pl.multiple_of(c * half, half), half), :] + got_c[...]

    streams = ((nx, x, peers_x, ny, y, peers_y), (ny, y, peers_y, nx, x, peers_x))
    waits = []
    for i, (n1, me1, peers1, _, _, _) in enumerate(streams):
        s, r = new_sems(n1 - 1), new_sems(n1 - 1)
        for q in range(1, n1):
            to = lax.rem(me1 + q, n1)
            src = acc.at[pl.ds(pl.multiple_of(i * stream + to * rows_1[i], 16), rows_1[i])]
            cp = copy(src, got_1.at[i, q - 1], s + q - 1, r + q - 1, peers1[q - 1])
            cp.start()
            waits.append(cp)
    for i, (n1, me1, _, _, _, _) in enumerate(streams):
        for cp in waits[i * (n1 - 1) : (i + 1) * (n1 - 1)]:
            cp.wait_recv()
        v = acc[pl.ds(pl.multiple_of(i * stream + me1 * rows_1[i], 16), rows_1[i]), :]
        for q in range(n1 - 1):
            v = v + got_1[i, q]
        mid[i] = v
    sent += waits

    waits = []
    for i, (_, _, _, n2, me2, peers2) in enumerate(streams):
        s, r = new_sems(n2 - 1), new_sems(n2 - 1)
        for q in range(1, n2):
            to = lax.rem(me2 + q, n2)
            src = mid.at[i, pl.ds(pl.multiple_of(to * rows_2, 16), rows_2)]
            cp = copy(src, got_2.at[i, q - 1], s + q - 1, r + q - 1, peers2[q - 1])
            cp.start()
            waits.append(cp)
    for i, (_, _, _, n2, me2, _) in enumerate(streams):
        for cp in waits[i * (n2 - 1) : (i + 1) * (n2 - 1)]:
            cp.wait_recv()
        v = mid[i, pl.ds(pl.multiple_of(me2 * rows_2, 16), rows_2), :]
        for q in range(n2 - 1):
            v = v + got_2[i, q]
        own[i * rows_2 : (i + 1) * rows_2, :] = v
    sent += waits

    owners = [(t * nz) // tiles for t in range(tiles)]
    bases = [c * half + x * rows_1[0] + y * rows_2, c * half + stream + y * rows_1[1] + x * rows_2]
    mine = (z * tiles + nz - 1) // nz
    is_owner = (mine * nz) // tiles == z
    half_tiles = tiles // 2
    s_z, r_z = new_sems(tiles), new_sems(nz - 1)

    def to_owner(t):
        slot = lax.rem(z - owners[t] + nz - 1 + nz, nz)
        return copy(own.at[pl.ds(t * tile, tile)], got_z.at[slot], s_z + t, r_z + slot, device(owners[t], y, x, c))

    for t in range(tiles):
        @pl.when(z != owners[t])
        def _():
            to_owner(t).start()

    def tile_rows(t, hi_half):
        base = jnp.where(hi_half, bases[1] + (t - half_tiles) * tile, bases[0] + t * tile)
        return pl.ds(pl.multiple_of(base, 16), tile)

    s_g, r_g = new_sems(nz - 1), new_sems(tiles)

    @pl.when(is_owner)
    def _():
        v = own[pl.ds(pl.multiple_of(mine * tile, 16), tile), :]
        for q in range(nz - 1):
            copy(own.at[pl.ds(0, tile)], got_z.at[q], s_z, r_z + q, other).wait_recv()
        for q in range(nz - 1):
            v = v + got_z[q]
        where = tile_rows(mine, mine >= half_tiles)
        total[where, :] = v
        for q in range(nz - 1):
            copy(total.at[where], total.at[where], s_g + q, r_g + mine, peers_z[q]).start()

    for t in range(tiles):
        i = t // half_tiles
        where = pl.ds(pl.multiple_of(bases[i] + (t - i * half_tiles) * tile, 16), tile)

        @pl.when(z != owners[t])
        def _():
            copy(total.at[where], total.at[where], s_g, r_g + t, other).wait_recv()

    waits = []
    for i, (_, _, _, n2, me2, peers2) in enumerate(streams):
        s, r = new_sems(n2 - 1), new_sems(n2 - 1)
        where = total.at[pl.ds(pl.multiple_of(bases[i], 16), rows_2)]
        for q in range(1, n2):
            cp = copy(where, where, s + q - 1, r + q - 1, peers2[q - 1])
            cp.start()
            waits.append(cp)
    for cp in waits:
        cp.wait_recv()
    sent += waits

    waits = []
    for i, (n1, me1, peers1, _, _, _) in enumerate(streams):
        s, r = new_sems(n1 - 1), new_sems(n1 - 1)
        where = total.at[pl.ds(pl.multiple_of(c * half + i * stream + me1 * rows_1[i], 16), rows_1[i])]
        for q in range(1, n1):
            cp = copy(where, where, s + q - 1, r + q - 1, peers1[q - 1])
            cp.start()
            waits.append(cp)
    for cp in waits:
        cp.wait_recv()
    sent += waits

    s, r = new_sems(1), new_sems(1)
    where = total.at[pl.ds(pl.multiple_of(c * half, half), half)]
    cp = copy(where, where, s, r, other)
    cp.start()
    cp.wait_recv()
    sent.append(cp)

    for cp in sent:
        cp.wait_send()
    for t in range(tiles):
        @pl.when(z != owners[t])
        def _():
            to_owner(t).wait_send()

    @pl.when(is_owner)
    def _():
        where = tile_rows(mine, mine >= half_tiles)
        for q in range(nz - 1):
            copy(total.at[where], total.at[where], s_g + q, r_g + mine, peers_z[q]).wait_send()


def passes_kernel(scale, slab_ref, total, basis_ref, factor_ref, g_high, g_low, w_high, w_low, p_pad):
    k, d = p_pad.shape[0] // 2, slab_ref.shape[1]
    nb = d // LANE

    at = 0
    for i in range(nb):
        for j in range(i, nb):
            v = total[at * LANE : (at + 1) * LANE, :]
            at += 1
            high, low = split(v)
            g_high[i * LANE : (i + 1) * LANE, j * LANE : (j + 1) * LANE] = high
            g_low[i * LANE : (i + 1) * LANE, j * LANE : (j + 1) * LANE] = low
            if j > i:
                high, low = split(v.T)
                g_high[j * LANE : (j + 1) * LANE, i * LANE : (i + 1) * LANE] = high
                g_low[j * LANE : (j + 1) * LANE, i * LANE : (i + 1) * LANE] = low

    w_high[0:k, :] = jnp.zeros((k, d), BF16)
    w_low[0:k, :] = jnp.zeros((k, d), BF16)
    p_pad[k : 2 * k, :] = jnp.zeros((k, d), BF16)
    current = jnp.concatenate(
        [total[at * LANE + j * k : at * LANE + (j + 1) * k, :] for j in range(nb)], axis=1
    )
    row = lax.broadcasted_iota(jnp.int32, (k, 2 * k), 0)
    col = lax.broadcasted_iota(jnp.int32, (k, 2 * k), 1)
    eye = jnp.where(col == row + k, 1.0, 0.0)
    for step in range(ITERS):
        pb = current.astype(BF16)
        p_pad[0:k, :] = pb
        wh, wl = split(dot(pb, g_high[...]) + dot(pb, g_low[...]))
        m = factor_rows(dot_t(wh, p_pad[...]) + dot_t(wl, p_pad[...]) + eye, k)
        mh, ml = split(m)
        if step < ITERS - 1:
            w_high[k : 2 * k, :] = wh
            w_low[k : 2 * k, :] = wl
            current = dot(mh, w_high[...]) + (dot(mh, w_low[...]) + dot(ml, w_high[...]))
        else:
            rows = slab_ref.shape[0]
            ih, il = split(dot_t(pb, slab_ref[...]))
            w_high[k : 2 * k, 0:rows] = ih
            w_low[k : 2 * k, 0:rows] = il
            ih, il = w_high[:, 0:rows], w_low[:, 0:rows]
            basis_ref[...] = (dot(mh, ih) + (dot(mh, il) + dot(ml, ih))) * scale
            factor_ref[...] = jnp.where(col >= row, m, 0.0)[:, 0:k] * (1.0 / scale)


def body(sizes, slab, panel):
    nz, ny, nx, tiles = sizes
    rows, d = slab.shape
    k = panel.shape[0]
    nb = d // LANE
    blocks = nb * (nb + 1) // 2 + nb * k // LANE
    half = blocks * LANE // CORES
    stream = half // 2
    rows_1, rows_2 = stream // nx, stream // (nx * ny)
    tile = 2 * rows_2 // tiles
    scale = math.sqrt(rows * nz * ny * nx * CORES)
    n_sems = 4 + 4 * (nx - 1 + ny - 1) * 2 + 2 * (tiles + nz - 1)
    params = functools.partial(pltpu.CompilerParams, vmem_limit_bytes=40 * 1024 * 1024)
    vmem = pl.BlockSpec(memory_space=pltpu.VMEM)
    total = pl.pallas_call(
        functools.partial(reduce_kernel, (nz, ny, nx), tiles),
        out_shape=jax.ShapeDtypeStruct((2 * half, LANE), F32),
        in_specs=[vmem] * 2,
        out_specs=vmem,
        scratch_shapes=[
            pltpu.VMEM((2 * half, LANE), F32),
            pltpu.VMEM((half, LANE), F32),
            pltpu.VMEM((half, LANE), F32),
            pltpu.VMEM((2, nx - 1, rows_1, LANE), F32),
            pltpu.VMEM((2, rows_1, LANE), F32),
            pltpu.VMEM((2, ny - 1, rows_2, LANE), F32),
            pltpu.VMEM((2 * rows_2, LANE), F32),
            pltpu.VMEM((nz - 1, tile, LANE), F32),
            pltpu.SemaphoreType.DMA((n_sems,)),
        ],
        compiler_params=params(collective_id=0, has_side_effects=True),
        cost_estimate=pl.CostEstimate(flops=10**9, bytes_accessed=10**7, transcendentals=0),
    )(slab, panel)
    return pl.pallas_call(
        functools.partial(passes_kernel, scale),
        out_shape=(jax.ShapeDtypeStruct((k, rows), F32), jax.ShapeDtypeStruct((k, k), F32)),
        in_specs=[vmem] * 2,
        out_specs=(vmem,) * 2,
        scratch_shapes=[
            pltpu.VMEM((d, d), BF16),
            pltpu.VMEM((d, d), BF16),
            pltpu.VMEM((2 * k, d), BF16),
            pltpu.VMEM((2 * k, d), BF16),
            pltpu.VMEM((2 * k, d), BF16),
        ],
        compiler_params=params(),
        cost_estimate=pl.CostEstimate(flops=2 * 10**9, bytes_accessed=3 * 10**6, transcendentals=0),
    )(slab, total)


def solution(mesh):
    nz = mesh.shape["rowa"]
    side = math.isqrt(mesh.shape["rowb"] // CORES)
    tiles = 10 if nz == 16 else 2
    in_specs = (P(("rowa", "rowb"), None), P(None, ("rowa", "rowb")))
    out_specs = (P(None, ("rowa", "rowb")), P())
    return jax.shard_map(
        functools.partial(body, (nz, side, side, tiles)),
        mesh=mesh, in_specs=in_specs, out_specs=out_specs, check_vma=False,
    )
```

```python
import functools
import math

import jax
import jax.numpy as jnp
from jax import lax
from jax.experimental import pallas as pl
from jax.experimental.pallas import tpu as pltpu
from jax.sharding import PartitionSpec as P

ITERS = 3
MESH = pl.DeviceIdType.MESH
F32 = jnp.float32
BF16 = jnp.bfloat16
LANE = 128
CORES = 2
PANEL = 4


def dot(a, b):
    return jnp.dot(a, b, preferred_element_type=F32)


def dot_t(a, b):
    return lax.dot_general(a, b, (((1,), (1,)), ((), ())), preferred_element_type=F32)


def split(v):
    high = v.astype(BF16)
    return high, (v - high.astype(F32)).astype(BF16)


def factor_rows(m, k):
    groups = [m[8 * i : 8 * i + 8, :] for i in range(k // 8)]
    full = groups[0].shape
    done = [[None] * 8 for _ in groups]
    for first in range(0, k, PANEL):
        g, s = divmod(first, 8)
        size = range(PANEL)
        rows = [jnp.broadcast_to(groups[g][s + q : s + q + 1, :], full) for q in size]
        cols = [
            {i: jnp.broadcast_to(groups[i][:, first + q : first + q + 1], full) for i in range(g, len(groups))}
            for q in size
        ]
        piv = [[jnp.broadcast_to(cols[r][g][s + q : s + q + 1, :], full) for r in size] for q in size]
        inv = []
        for q in size:
            inv.append(1.0 / piv[q][q])
            for r in range(q + 1, PANEL):
                t = piv[q][r] * inv[q]
                rows[r] = rows[r] - t * rows[q]
                for i in cols[r]:
                    cols[r][i] = cols[r][i] - t * cols[q][i]
                for w in range(r, PANEL):
                    piv[r][w] = piv[r][w] - t * piv[q][w]
            done[g][s + q] = rows[q] * lax.rsqrt(piv[q][q])
        for i in range(g, len(groups)):
            new = groups[i]
            for q in size:
                new = new - (cols[q][i] * inv[q]) * rows[q]
            groups[i] = new
    sub = lax.broadcasted_iota(jnp.int32, full, 0)
    out = []
    for rows in done:
        v = rows[0]
        for q in range(1, 8):
            v = jnp.where(sub == q, rows[q], v)
        out.append(v)
    return jnp.concatenate(out, axis=0)


JOBS = (
    (
        (("g", 0, 0, 8), ("g", 3, 3, 8), ("g", 4, 4, 8), ("g", 7, 7, 8), ("p", 0, 4)),
        (("g", 1, 1, 8), ("g", 2, 2, 8), ("g", 5, 5, 8), ("g", 6, 6, 8), ("p", 4, 8)),
    ),
)
CHUNKS = len(JOBS)
Z_GROUP = 8
ROWS = (20 * LANE,)


def places(ch, cc, k):
    at, out = 0, []
    for job in JOBS[ch][cc]:
        for j in range(job[-2], job[-1]):
            out.append((job[0], job[1] if job[0] == "g" else 0, j, at))
            at += LANE if job[0] == "g" else k
    return out


def z_tiles(ch):
    mine = ROWS[ch] // 32
    tile = 8 if mine <= 8 * Z_GROUP else 16
    return mine // tile, tile


def flip(bit, mask):
    return bit + mask - 2 * bit * mask


def reduce_kernel(dims, slab, panel, g_high, g_low, first, slab_2, panel_2, *refs):
    part, got_1, got_2, own, got_z, own_t, total = (refs[i * CHUNKS : (i + 1) * CHUNKS] for i in range(7))
    (sems,) = refs[7 * CHUNKS :]
    slabs, panels = (slab, slab_2), (panel, panel_2)
    nz, ny, nx = dims
    k = panel.shape[0]

    z = lax.axis_index("rowa")
    b = lax.axis_index("rowb")
    c = lax.rem(b, CORES)
    x = lax.rem(b // CORES, nx)
    y = b // (CORES * nx)

    def device(zz, yy, xx, cc):
        return (zz, (yy * nx + xx) * CORES + cc)

    def ring_pairs(i, n):
        low = lax.rem(i, 2)
        return (lax.rem((i + 1) // 2, 2), i + 1 - 2 * low), (i // 2, n - 1 - i)

    pair_x, pair_y = ring_pairs(x, nx), ring_pairs(y, ny)
    z_bit, z_at = lax.rem(z, 2), z // 2
    pair_z = (z_bit, z + 1 - 2 * z_bit), (z_bit, lax.rem(z - 1 + 2 * z_bit + nz, nz))

    def cube(which, mask):
        return device(
            pair_z[which][1] if mask & 4 else z,
            pair_y[which][1] if mask & 2 else y,
            pair_x[which][1] if mask & 1 else x,
            c,
        )

    def index(which, mask, size):
        at = flip(pair_x[which][0], mask & 1) + 2 * flip(pair_y[which][0], mask // 2 & 1)
        return at + 4 * flip(pair_z[which][0], mask // 4) if size == 8 else at

    other = device(z, y, x, 1 - c)
    peers_z = [device(2 * lax.rem(z_at + q, Z_GROUP) + z_bit, y, x, c) for q in range(1, Z_GROUP)]

    barrier = pltpu.get_barrier_semaphore()
    everyone = [other] + [cube(s, m) for s in range(2) for m in range(1, 8)] + peers_z
    for peer in everyone:
        pl.semaphore_signal(barrier, inc=1, device_id=peer, device_id_type=MESH)

    used = [0]

    def new_sems(count):
        used[0] += count
        return used[0] - count

    def copy(src, dst, send, recv, peer):
        return pltpu.make_async_remote_copy(
            src_ref=src, dst_ref=dst, send_sem=sems.at[send], recv_sem=sems.at[recv], device_id=peer, device_id_type=MESH
        )

    sent = []
    pl.semaphore_wait(barrier, len(everyone))

    at = new_sems(4)
    exchange = [
        copy(slab, slab_2, at, at + 1, other),
        copy(panel, panel_2, at + 2, at + 3, other),
    ]
    for cp in exchange:
        cp.start()
    sent += exchange

    def work(ch, which):
        for cc in range(CORES):
            @pl.when(c == cc)
            def _():
                at = 0
                for job in JOBS[ch][cc]:
                    j0, j1 = job[-2:]
                    if job[0] == "g":
                        left, step = slabs[which][:, job[1] * LANE : (job[1] + 1) * LANE].T, LANE
                    else:
                        left, step = panels[which][...], k
                    v = dot(left, slabs[which][:, j0 * LANE : j1 * LANE])
                    for j in range(j1 - j0):
                        new = v[:, j * LANE : (j + 1) * LANE]
                        if which:
                            new = part[ch][at : at + step, :] + new
                        part[ch][at : at + step, :] = new
                        at += step

    def steps(ch):
        size = ROWS[ch] // 2
        piece, last = size // 8, size // 32
        tiles, tile = z_tiles(ch)
        owners = [((t * Z_GROUP) // tiles + ch) % Z_GROUP for t in range(tiles)]
        spot = lax.rem(z_at - ch + Z_GROUP, Z_GROUP)
        mine = (spot * tiles + Z_GROUP - 1) // Z_GROUP
        is_owner = (mine * Z_GROUP) // tiles == spot
        started = {}

        def rows(off, count):
            return pl.ds(off if isinstance(off, int) else pl.multiple_of(off, 8), count)

        off_1 = [s * size + index(s, 0, 8) * piece for s in range(2)]
        off_2 = [off_1[s] + index(1 - s, 0, 4) * last for s in range(2)]

        def start(key, src, dst, peer):
            at = new_sems(2)
            cp = started[key] = copy(src, dst, at, at + 1, peer)
            cp.start()
            sent.append(cp)

        def begin():
            for s in range(2):
                for m in range(1, 8):
                    src = part[ch].at[rows(s * size + index(s, m, 8) * piece, piece)]
                    start(("r1", s, m), src, got_1[ch].at[s, m - 1], cube(s, m))

        def second():
            for s in range(2):
                v = part[ch][rows(off_1[s], piece), :]
                for m in range(1, 8):
                    started["r1", s, m].wait_recv()
                    v = v + got_1[ch][s, m - 1]
                part[ch][rows(off_1[s], piece), :] = v
                for m in range(1, 4):
                    src = part[ch].at[rows(off_1[s] + index(1 - s, m, 4) * last, last)]
                    start(("r2", s, m), src, got_2[ch].at[s, m - 1], cube(1 - s, m))

        s_z, r_z, s_g, r_g = new_sems(tiles), new_sems(Z_GROUP - 1), new_sems(Z_GROUP - 1), new_sems(tiles)

        def to_owner(t):
            slot = lax.rem(z_at - owners[t] + 2 * Z_GROUP - 1, Z_GROUP)
            src = own[ch].at[pl.ds(t * tile, tile)]
            return copy(src, got_z[ch].at[slot], s_z + t, r_z + slot, device(2 * owners[t] + z_bit, y, x, c))

        def to_all(q):
            where = own_t[ch].at[rows(mine * tile, tile)]
            return copy(where, where, s_g + q, r_g + mine, peers_z[q])

        def to_z():
            for s in range(2):
                v = part[ch][rows(off_2[s], last), :]
                for m in range(1, 4):
                    started["r2", s, m].wait_recv()
                    v = v + got_2[ch][s, m - 1]
                own[ch][s * last : (s + 1) * last, :] = v
            for t in range(tiles):
                @pl.when(z_at != owners[t])
                def _():
                    to_owner(t).start()

        def at_owner():
            @pl.when(is_owner)
            def _():
                v = own[ch][rows(mine * tile, tile), :]
                for q in range(Z_GROUP - 1):
                    copy(own[ch].at[pl.ds(0, tile)], got_z[ch].at[q], s_z, r_z + q, other).wait_recv()
                    v = v + got_z[ch][q]
                own_t[ch][rows(mine * tile, tile), :] = v
                for q in range(Z_GROUP - 1):
                    to_all(q).start()

        def from_z():
            for t in range(tiles):
                where = own_t[ch].at[pl.ds(t * tile, tile)]

                @pl.when(z_at != owners[t])
                def _():
                    copy(where, where, s_g, r_g + t, other).wait_recv()
            for s in range(2):
                where = rows(off_2[s], last)
                for m in range(1, 4):
                    start(("g2", s, m), own_t[ch].at[pl.ds(s * last, last)], total[ch].at[c, where], cube(1 - s, m))
                total[ch][c, where, :] = own_t[ch][s * last : (s + 1) * last, :]

        def gather():
            for s in range(2):
                for m in range(1, 4):
                    started["g2", s, m].wait_recv()
                where = total[ch].at[c, rows(off_1[s], piece)]
                for m in range(1, 8):
                    start(("g1", s, m), where, where, cube(s, m))

        def across():
            for s in range(2):
                for m in range(1, 8):
                    started["g1", s, m].wait_recv()
                where = total[ch].at[c, pl.ds(s * size, size)]
                start(("c", s), where, where, other)

        def finish():
            for s in range(2):
                started["c", s].wait_recv()
            for cc in range(CORES):
                for kind, i, j, at in places(ch, cc, k):
                    if kind == "p":
                        first[:, j * LANE : (j + 1) * LANE] = total[ch][cc, at : at + k, :]
                        continue
                    v = total[ch][cc, at : at + LANE, :]
                    for a, e, w in ((i, j, v), (j, i, v.T))[: 2 if j > i else 1]:
                        high, low = split(w)
                        g_high[a * LANE : (a + 1) * LANE, e * LANE : (e + 1) * LANE] = high
                        g_low[a * LANE : (a + 1) * LANE, e * LANE : (e + 1) * LANE] = low

        def drain():
            for t in range(tiles):
                @pl.when(z_at != owners[t])
                def _():
                    to_owner(t).wait_send()

            @pl.when(is_owner)
            def _():
                for q in range(Z_GROUP - 1):
                    to_all(q).wait_send()

        return begin, (second, to_z, at_owner, from_z, gather, across, finish), drain

    chunks = [steps(ch) for ch in range(CHUNKS)]
    for ch in range(CHUNKS):
        work(ch, 0)
    for cp in exchange:
        cp.wait_recv()
    for ch in range(CHUNKS):
        work(ch, 1)
        chunks[ch][0]()
    for at in range(len(chunks[0][1])):
        for ch in range(CHUNKS):
            chunks[ch][1][at]()
    for cp in sent:
        cp.wait_send()
    for ch in range(CHUNKS):
        chunks[ch][2]()


def passes_kernel(scale, slab, g_high, g_low, first, basis_ref, factor_ref, w_high, w_low, p_pad):
    k, d = first.shape
    w_high[0:k, :] = jnp.zeros((k, d), BF16)
    w_low[0:k, :] = jnp.zeros((k, d), BF16)
    p_pad[k : 2 * k, :] = jnp.zeros((k, d), BF16)
    current = first[...]
    row = lax.broadcasted_iota(jnp.int32, (k, 2 * k), 0)
    col = lax.broadcasted_iota(jnp.int32, (k, 2 * k), 1)
    eye = jnp.where(col == row + k, 1.0, 0.0)
    for step in range(ITERS):
        pb = current.astype(BF16)
        p_pad[0:k, :] = pb
        wh, wl = split(dot(pb, g_high[...]) + dot(pb, g_low[...]))
        m = factor_rows(dot_t(wh, p_pad[...]) + dot_t(wl, p_pad[...]) + eye, k)
        mh, ml = split(m)
        if step < ITERS - 1:
            w_high[k : 2 * k, :] = wh
            w_low[k : 2 * k, :] = wl
            current = dot(mh, w_high[...]) + (dot(mh, w_low[...]) + dot(ml, w_high[...]))
        else:
            rows = slab.shape[0]
            ih, il = split(dot_t(pb, slab[...]))
            w_high[k : 2 * k, 0:rows] = ih
            w_low[k : 2 * k, 0:rows] = il
            ih, il = w_high[:, 0:rows], w_low[:, 0:rows]
            basis_ref[...] = (dot(mh, ih) + (dot(mh, il) + dot(ml, ih))) * scale
            factor_ref[...] = jnp.where(col >= row, m, 0.0)[:, 0:k] * (1.0 / scale)


def body(sizes, slab, panel):
    nz, ny, nx = sizes
    rows, d = slab.shape
    k = panel.shape[0]
    scale = math.sqrt(rows * nz * ny * nx * CORES)
    tiles = [z_tiles(ch) for ch in range(CHUNKS)]
    n_sems = 4 + sum(4 * (7 + 3) * 2 + 2 * (t + Z_GROUP - 1) + 4 for t, _ in tiles)
    params = functools.partial(pltpu.CompilerParams, vmem_limit_bytes=36 * 1024 * 1024)
    vmem = pl.BlockSpec(memory_space=pltpu.VMEM)

    def each(shape):
        return [pltpu.VMEM(shape(ch), F32) for ch in range(CHUNKS)]

    g_high, g_low, first = pl.pallas_call(
        functools.partial(reduce_kernel, (nz, ny, nx)),
        out_shape=(
            jax.ShapeDtypeStruct((d, d), BF16), jax.ShapeDtypeStruct((d, d), BF16), jax.ShapeDtypeStruct((k, d), F32)
        ),
        in_specs=[vmem] * 2,
        out_specs=(vmem,) * 3,
        scratch_shapes=[
            pltpu.VMEM((rows, d), BF16),
            pltpu.VMEM((k, rows), BF16),
            *each(lambda ch: (ROWS[ch], LANE)),
            *each(lambda ch: (2, 7, ROWS[ch] // 16, LANE)),
            *each(lambda ch: (2, 3, ROWS[ch] // 64, LANE)),
            *each(lambda ch: (ROWS[ch] // 32, LANE)),
            *each(lambda ch: (Z_GROUP - 1, tiles[ch][1], LANE)),
            *each(lambda ch: (ROWS[ch] // 32, LANE)),
            *each(lambda ch: (CORES, ROWS[ch], LANE)),
            pltpu.SemaphoreType.DMA((n_sems,)),
        ],
        compiler_params=params(collective_id=0, has_side_effects=True),
        cost_estimate=pl.CostEstimate(flops=10**9, bytes_accessed=10**7, transcendentals=0),
    )(slab, panel)
    return pl.pallas_call(
        functools.partial(passes_kernel, scale),
        out_shape=(jax.ShapeDtypeStruct((k, rows), F32), jax.ShapeDtypeStruct((k, k), F32)),
        in_specs=[vmem] * 4,
        out_specs=(vmem,) * 2,
        scratch_shapes=[
            pltpu.VMEM((2 * k, d), BF16),
            pltpu.VMEM((2 * k, d), BF16),
            pltpu.VMEM((2 * k, d), BF16),
        ],
        compiler_params=params(),
        cost_estimate=pl.CostEstimate(flops=2 * 10**9, bytes_accessed=3 * 10**6, transcendentals=0),
    )(slab, g_high, g_low, first)


def solution(mesh):
    nz = mesh.shape["rowa"]
    side = math.isqrt(mesh.shape["rowb"] // CORES)
    in_specs = (P(("rowa", "rowb"), None), P(None, ("rowa", "rowb")))
    out_specs = (P(None, ("rowa", "rowb")), P())
    return jax.shard_map(
        functools.partial(body, (nz, side, side)),
        mesh=mesh, in_specs=in_specs, out_specs=out_specs, check_vma=False,
    )
```

```python
import functools
import math

import jax
import jax.numpy as jnp
from jax import lax
from jax.experimental import pallas as pl
from jax.experimental.pallas import tpu as pltpu
from jax.sharding import PartitionSpec as P

ITERS = 3
MESH = pl.DeviceIdType.MESH
F32 = jnp.float32
BF16 = jnp.bfloat16
LANE = 128
CORES = 2
PANEL = 8


def dot(a, b):
    return jnp.dot(a, b, preferred_element_type=F32)


def dot_t(a, b):
    return lax.dot_general(a, b, (((1,), (1,)), ((), ())), preferred_element_type=F32)


def split(v):
    high = v.astype(BF16)
    return high, (v - high.astype(F32)).astype(BF16)


def factor_rows(m, k):
    groups = [m[8 * i : 8 * i + 8, :] for i in range(k // 8)]
    full = groups[0].shape
    done = [[None] * 8 for _ in groups]
    for first in range(0, k, PANEL):
        g, s = divmod(first, 8)
        size = range(PANEL)
        rows = [jnp.broadcast_to(groups[g][s + q : s + q + 1, :], full) for q in size]
        cols = [
            {i: jnp.broadcast_to(groups[i][:, first + q : first + q + 1], full) for i in range(g, len(groups))}
            for q in size
        ]
        piv = [[jnp.broadcast_to(cols[r][g][s + q : s + q + 1, :], full) for r in size] for q in size]
        inv = []
        for q in size:
            inv.append(pl.reciprocal(piv[q][q]))
            for r in range(q + 1, PANEL):
                t = piv[q][r] * inv[q]
                rows[r] = rows[r] - t * rows[q]
                for i in cols[r]:
                    cols[r][i] = cols[r][i] - t * cols[q][i]
                for w in range(r, PANEL):
                    piv[r][w] = piv[r][w] - t * piv[q][w]
            done[g][s + q] = rows[q] * lax.rsqrt(piv[q][q])
        for i in range(g, len(groups)):
            new = groups[i]
            for q in size:
                new = new - (cols[q][i] * inv[q]) * rows[q]
            groups[i] = new
    sub = lax.broadcasted_iota(jnp.int32, full, 0)
    out = []
    for rows in done:
        v = rows[0]
        for q in range(1, 8):
            v = jnp.where(sub == q, rows[q], v)
        out.append(v)
    return jnp.concatenate(out, axis=0)


JOBS = (
    ((("g", 0, 0, 8),), (("g", 2, 2, 8), ("g", 6, 6, 8))),
    ((("g", 3, 3, 8), ("g", 4, 4, 8), ("g", 7, 7, 8), ("p", 0, 4)), (("g", 1, 1, 8), ("g", 5, 5, 8), ("p", 4, 8))),
)
CHUNKS = len(JOBS)
Z_GROUP = 8
ROWS = (8 * LANE, 12 * LANE)


def places(ch, cc, k):
    at, out = 0, []
    for job in JOBS[ch][cc]:
        for j in range(job[-2], job[-1]):
            out.append((job[0], job[1] if job[0] == "g" else 0, j, at))
            at += LANE if job[0] == "g" else k
    return out


def z_tiles(ch):
    mine = ROWS[ch] // 32
    tile = 8 if mine <= 8 * Z_GROUP else 16
    return mine // tile, tile


def flip(bit, mask):
    return bit + mask - 2 * bit * mask


def reduce_kernel(dims, slab, panel, g_high, g_low, first, slab_2, panel_2, *refs):
    part, got_1, got_2, own, got_z, own_t, total = (refs[i * CHUNKS : (i + 1) * CHUNKS] for i in range(7))
    (sems,) = refs[7 * CHUNKS :]
    slabs, panels = (slab, slab_2), (panel, panel_2)
    nz, ny, nx = dims
    k = panel.shape[0]

    z = lax.axis_index("rowa")
    b = lax.axis_index("rowb")
    c = lax.rem(b, CORES)
    x = lax.rem(b // CORES, nx)
    y = b // (CORES * nx)

    def device(zz, yy, xx, cc):
        return (zz, (yy * nx + xx) * CORES + cc)

    def ring_pairs(i, n):
        low = lax.rem(i, 2)
        return (lax.rem((i + 1) // 2, 2), i + 1 - 2 * low), (i // 2, n - 1 - i)

    pair_x, pair_y = ring_pairs(x, nx), ring_pairs(y, ny)
    z_bit, z_at = lax.rem(z, 2), z // 2
    pair_z = (z_bit, z + 1 - 2 * z_bit), (z_bit, lax.rem(z - 1 + 2 * z_bit + nz, nz))

    def cube(which, mask):
        return device(
            pair_z[which][1] if mask & 4 else z,
            pair_y[which][1] if mask & 2 else y,
            pair_x[which][1] if mask & 1 else x,
            c,
        )

    def index(which, mask, size):
        at = flip(pair_x[which][0], mask & 1) + 2 * flip(pair_y[which][0], mask // 2 & 1)
        return at + 4 * flip(pair_z[which][0], mask // 4) if size == 8 else at

    other = device(z, y, x, 1 - c)
    peers_z = [device(2 * lax.rem(z_at + q, Z_GROUP) + z_bit, y, x, c) for q in range(1, Z_GROUP)]

    barrier = pltpu.get_barrier_semaphore()
    everyone = [other] + [cube(s, m) for s in range(2) for m in range(1, 8)] + peers_z
    for peer in everyone:
        pl.semaphore_signal(barrier, inc=1, device_id=peer, device_id_type=MESH)

    used = [0]

    def new_sems(count):
        used[0] += count
        return used[0] - count

    def copy(src, dst, send, recv, peer):
        return pltpu.make_async_remote_copy(
            src_ref=src, dst_ref=dst, send_sem=sems.at[send], recv_sem=sems.at[recv], device_id=peer, device_id_type=MESH
        )

    sent = []
    pl.semaphore_wait(barrier, len(everyone))

    at = new_sems(4)
    exchange = [
        copy(slab, slab_2, at, at + 1, other),
        copy(panel, panel_2, at + 2, at + 3, other),
    ]
    for cp in exchange:
        cp.start()
    sent += exchange

    def work(ch, which):
        for cc in range(CORES):
            @pl.when(c == cc)
            def _():
                at = 0
                for job in JOBS[ch][cc]:
                    j0, j1 = job[-2:]
                    if job[0] == "g":
                        left, step = slabs[which][:, job[1] * LANE : (job[1] + 1) * LANE].T, LANE
                    else:
                        left, step = panels[which][...], k
                    v = dot(left, slabs[which][:, j0 * LANE : j1 * LANE])
                    for j in range(j1 - j0):
                        new = v[:, j * LANE : (j + 1) * LANE]
                        if which:
                            new = part[ch][at : at + step, :] + new
                        part[ch][at : at + step, :] = new
                        at += step

    def steps(ch):
        size = ROWS[ch] // 2
        piece, last = size // 8, size // 32
        tiles, tile = z_tiles(ch)
        owners = [((t * Z_GROUP) // tiles + ch) % Z_GROUP for t in range(tiles)]
        spot = lax.rem(z_at - ch + Z_GROUP, Z_GROUP)
        mine = (spot * tiles + Z_GROUP - 1) // Z_GROUP
        is_owner = (mine * Z_GROUP) // tiles == spot
        started = {}

        def rows(off, count):
            return pl.ds(off if isinstance(off, int) else pl.multiple_of(off, 8), count)

        off_1 = [s * size + index(s, 0, 8) * piece for s in range(2)]
        off_2 = [off_1[s] + index(1 - s, 0, 4) * last for s in range(2)]

        def start(key, src, dst, peer):
            at = new_sems(2)
            cp = started[key] = copy(src, dst, at, at + 1, peer)
            cp.start()
            sent.append(cp)

        def begin():
            for s in range(2):
                for m in range(1, 8):
                    src = part[ch].at[rows(s * size + index(s, m, 8) * piece, piece)]
                    start(("r1", s, m), src, got_1[ch].at[s, m - 1], cube(s, m))

        def second():
            for s in range(2):
                v = part[ch][rows(off_1[s], piece), :]
                for m in range(1, 8):
                    started["r1", s, m].wait_recv()
                    v = v + got_1[ch][s, m - 1]
                part[ch][rows(off_1[s], piece), :] = v
                for m in range(1, 4):
                    src = part[ch].at[rows(off_1[s] + index(1 - s, m, 4) * last, last)]
                    start(("r2", s, m), src, got_2[ch].at[s, m - 1], cube(1 - s, m))

        s_z, r_z, s_g, r_g = new_sems(tiles), new_sems(Z_GROUP - 1), new_sems(Z_GROUP - 1), new_sems(tiles)

        def to_owner(t):
            slot = lax.rem(z_at - owners[t] + 2 * Z_GROUP - 1, Z_GROUP)
            src = own[ch].at[pl.ds(t * tile, tile)]
            return copy(src, got_z[ch].at[slot], s_z + t, r_z + slot, device(2 * owners[t] + z_bit, y, x, c))

        def to_all(q):
            where = own_t[ch].at[rows(mine * tile, tile)]
            return copy(where, where, s_g + q, r_g + mine, peers_z[q])

        def to_z():
            for s in range(2):
                v = part[ch][rows(off_2[s], last), :]
                for m in range(1, 4):
                    started["r2", s, m].wait_recv()
                    v = v + got_2[ch][s, m - 1]
                own[ch][s * last : (s + 1) * last, :] = v
            for t in range(tiles):
                @pl.when(z_at != owners[t])
                def _():
                    to_owner(t).start()

        def at_owner():
            @pl.when(is_owner)
            def _():
                v = own[ch][rows(mine * tile, tile), :]
                for q in range(Z_GROUP - 1):
                    copy(own[ch].at[pl.ds(0, tile)], got_z[ch].at[q], s_z, r_z + q, other).wait_recv()
                    v = v + got_z[ch][q]
                own_t[ch][rows(mine * tile, tile), :] = v
                for q in range(Z_GROUP - 1):
                    to_all(q).start()

        def from_z():
            for t in range(tiles):
                where = own_t[ch].at[pl.ds(t * tile, tile)]

                @pl.when(z_at != owners[t])
                def _():
                    copy(where, where, s_g, r_g + t, other).wait_recv()
            for s in range(2):
                where = rows(off_2[s], last)
                for m in range(1, 4):
                    start(("g2", s, m), own_t[ch].at[pl.ds(s * last, last)], total[ch].at[c, where], cube(1 - s, m))
                total[ch][c, where, :] = own_t[ch][s * last : (s + 1) * last, :]

        def gather():
            for s in range(2):
                for m in range(1, 4):
                    started["g2", s, m].wait_recv()
                where = total[ch].at[c, rows(off_1[s], piece)]
                for m in range(1, 8):
                    start(("g1", s, m), where, where, cube(s, m))

        def across():
            for s in range(2):
                for m in range(1, 8):
                    started["g1", s, m].wait_recv()
                where = total[ch].at[c, pl.ds(s * size, size)]
                start(("c", s), where, where, other)

        def finish():
            for s in range(2):
                started["c", s].wait_recv()
            for cc in range(CORES):
                for kind, i, j, at in places(ch, cc, k):
                    if kind == "p":
                        first[:, j * LANE : (j + 1) * LANE] = total[ch][cc, at : at + k, :]
                        continue
                    v = total[ch][cc, at : at + LANE, :]
                    for a, e, w in ((i, j, v), (j, i, v.T))[: 2 if j > i else 1]:
                        high, low = split(w)
                        g_high[a * LANE : (a + 1) * LANE, e * LANE : (e + 1) * LANE] = high
                        g_low[a * LANE : (a + 1) * LANE, e * LANE : (e + 1) * LANE] = low

        def drain():
            for t in range(tiles):
                @pl.when(z_at != owners[t])
                def _():
                    to_owner(t).wait_send()

            @pl.when(is_owner)
            def _():
                for q in range(Z_GROUP - 1):
                    to_all(q).wait_send()

        return begin, (second, to_z, at_owner, from_z, gather, across, finish), drain

    chunks = [steps(ch) for ch in range(CHUNKS)]
    for ch in range(CHUNKS):
        work(ch, 0)
    for cp in exchange:
        cp.wait_recv()
    for ch in range(CHUNKS):
        work(ch, 1)
        chunks[ch][0]()
    count = len(chunks[0][1])
    for at in range(count + CHUNKS - 1):
        for ch in range(CHUNKS):
            if 0 <= at - ch < count:
                chunks[ch][1][at - ch]()
    for cp in sent:
        cp.wait_send()
    for ch in range(CHUNKS):
        chunks[ch][2]()


def passes_kernel(scale, slab, g_high, g_low, first, basis_ref, factor_ref, w_high, w_low, p_pad):
    k, d = first.shape
    w_high[0:k, :] = jnp.zeros((k, d), BF16)
    w_low[0:k, :] = jnp.zeros((k, d), BF16)
    p_pad[k : 2 * k, :] = jnp.zeros((k, d), BF16)
    current = first[...]
    row = lax.broadcasted_iota(jnp.int32, (k, 2 * k), 0)
    col = lax.broadcasted_iota(jnp.int32, (k, 2 * k), 1)
    eye = jnp.where(col == row + k, 1.0, 0.0)
    for step in range(ITERS):
        pb = current.astype(BF16)
        p_pad[0:k, :] = pb
        wh, wl = split(dot(pb, g_high[...]) + dot(pb, g_low[...]))
        if step == ITERS - 1:
            rows = slab.shape[0]
            ih, il = split(dot_t(pb, slab[...]))
        m = factor_rows(dot_t(wh, p_pad[...]) + dot_t(wl, p_pad[...]) + eye, k)
        mh, ml = split(m)
        if step < ITERS - 1:
            w_high[k : 2 * k, :] = wh
            w_low[k : 2 * k, :] = wl
            current = dot(mh, w_high[...]) + (dot(mh, w_low[...]) + dot(ml, w_high[...]))
        else:
            w_high[k : 2 * k, 0:rows] = ih
            w_low[k : 2 * k, 0:rows] = il
            ih, il = w_high[:, 0:rows], w_low[:, 0:rows]
            basis_ref[...] = (dot(mh, ih) + (dot(mh, il) + dot(ml, ih))) * scale
            factor_ref[...] = jnp.where(col >= row, m, 0.0)[:, 0:k] * (1.0 / scale)


def body(sizes, slab, panel):
    nz, ny, nx = sizes
    rows, d = slab.shape
    k = panel.shape[0]
    scale = math.sqrt(rows * nz * ny * nx * CORES)
    tiles = [z_tiles(ch) for ch in range(CHUNKS)]
    n_sems = 4 + sum(4 * (7 + 3) * 2 + 2 * (t + Z_GROUP - 1) + 4 for t, _ in tiles)
    params = functools.partial(pltpu.CompilerParams, vmem_limit_bytes=36 * 1024 * 1024)
    vmem = pl.BlockSpec(memory_space=pltpu.VMEM)

    def each(shape):
        return [pltpu.VMEM(shape(ch), F32) for ch in range(CHUNKS)]

    g_high, g_low, first = pl.pallas_call(
        functools.partial(reduce_kernel, (nz, ny, nx)),
        out_shape=(
            jax.ShapeDtypeStruct((d, d), BF16), jax.ShapeDtypeStruct((d, d), BF16), jax.ShapeDtypeStruct((k, d), F32)
        ),
        in_specs=[vmem] * 2,
        out_specs=(vmem,) * 3,
        scratch_shapes=[
            pltpu.VMEM((rows, d), BF16),
            pltpu.VMEM((k, rows), BF16),
            *each(lambda ch: (ROWS[ch], LANE)),
            *each(lambda ch: (2, 7, ROWS[ch] // 16, LANE)),
            *each(lambda ch: (2, 3, ROWS[ch] // 64, LANE)),
            *each(lambda ch: (ROWS[ch] // 32, LANE)),
            *each(lambda ch: (Z_GROUP - 1, tiles[ch][1], LANE)),
            *each(lambda ch: (ROWS[ch] // 32, LANE)),
            *each(lambda ch: (CORES, ROWS[ch], LANE)),
            pltpu.SemaphoreType.DMA((n_sems,)),
        ],
        compiler_params=params(collective_id=0, has_side_effects=True),
        cost_estimate=pl.CostEstimate(flops=10**9, bytes_accessed=10**7, transcendentals=0),
    )(slab, panel)
    return pl.pallas_call(
        functools.partial(passes_kernel, scale),
        out_shape=(jax.ShapeDtypeStruct((k, rows), F32), jax.ShapeDtypeStruct((k, k), F32)),
        in_specs=[vmem] * 4,
        out_specs=(vmem,) * 2,
        scratch_shapes=[
            pltpu.VMEM((2 * k, d), BF16),
            pltpu.VMEM((2 * k, d), BF16),
            pltpu.VMEM((2 * k, d), BF16),
        ],
        compiler_params=params(),
        cost_estimate=pl.CostEstimate(flops=2 * 10**9, bytes_accessed=3 * 10**6, transcendentals=0),
    )(slab, g_high, g_low, first)


def solution(mesh):
    nz = mesh.shape["rowa"]
    side = math.isqrt(mesh.shape["rowb"] // CORES)
    in_specs = (P(("rowa", "rowb"), None), P(None, ("rowa", "rowb")))
    out_specs = (P(None, ("rowa", "rowb")), P())
    return jax.shard_map(
        functools.partial(body, (nz, side, side)),
        mesh=mesh, in_specs=in_specs, out_specs=out_specs, check_vma=False,
    )
```

```python
import functools
import math

import jax
import jax.numpy as jnp
from jax import lax
from jax.experimental import pallas as pl
from jax.experimental.pallas import tpu as pltpu
from jax.sharding import PartitionSpec as P

ITERS = 3
MESH = pl.DeviceIdType.MESH
F32 = jnp.float32
BF16 = jnp.bfloat16
LANE = 128
CORES = 2
PANEL = 8


def dot(a, b):
    return jnp.dot(a, b, preferred_element_type=F32)


def dot_t(a, b):
    return lax.dot_general(a, b, (((1,), (1,)), ((), ())), preferred_element_type=F32)


def split(v):
    high = v.astype(BF16)
    return high, (v - high.astype(F32)).astype(BF16)


def factor_rows(m, k):
    groups = [m[8 * i : 8 * i + 8, :] for i in range(k // 8)]
    full = groups[0].shape
    done = [[None] * 8 for _ in groups]
    for first in range(0, k, PANEL):
        g, s = divmod(first, 8)
        size = range(PANEL)
        rows = [jnp.broadcast_to(groups[g][s + q : s + q + 1, :], full) for q in size]
        cols = [
            {i: jnp.broadcast_to(groups[i][:, first + q : first + q + 1], full) for i in range(g, len(groups))}
            for q in size
        ]
        piv = [[jnp.broadcast_to(cols[r][g][s + q : s + q + 1, :], full) for r in size] for q in size]
        inv = []
        for q in size:
            inv.append(pl.reciprocal(piv[q][q]))
            for r in range(q + 1, PANEL):
                t = piv[q][r] * inv[q]
                rows[r] = rows[r] - t * rows[q]
                for i in cols[r]:
                    cols[r][i] = cols[r][i] - t * cols[q][i]
                for w in range(r, PANEL):
                    piv[r][w] = piv[r][w] - t * piv[q][w]
            done[g][s + q] = rows[q] * lax.rsqrt(piv[q][q])
        for i in range(g, len(groups)):
            new = groups[i]
            for q in size:
                new = new - (cols[q][i] * inv[q]) * rows[q]
            groups[i] = new
    sub = lax.broadcasted_iota(jnp.int32, full, 0)
    out = []
    for rows in done:
        v = rows[0]
        for q in range(1, 8):
            v = jnp.where(sub == q, rows[q], v)
        out.append(v)
    return jnp.concatenate(out, axis=0)


JOBS = (
    (("g", 0, 0, 8), ("g", 3, 3, 8), ("g", 4, 4, 8), ("g", 7, 7, 8), ("p", 0, 4)),
    (("g", 1, 1, 8), ("g", 2, 2, 8), ("g", 5, 5, 8), ("g", 6, 6, 8), ("p", 4, 8)),
)
SIZES = (12 * LANE, 8 * LANE)
FIRST = (0, SIZES[0])
HALF = sum(SIZES)
PIECE = tuple(size // 8 for size in SIZES)
LAST = tuple(size // 64 for size in SIZES)
LAST_AT = (0, LAST[0])
OWN = sum(LAST)
FAR = 4


def places(cc, k):
    at, out = 0, []
    for job in JOBS[cc]:
        for j in range(job[-2], job[-1]):
            out.append((job[0], job[1] if job[0] == "g" else 0, j, at))
            at += LANE if job[0] == "g" else k
    return out


def flip(bit, mask):
    return bit + mask - 2 * bit * mask


def reduce_kernel(dims, slab, panel, g_high, g_low, first, part, got_c, got_1, got_2, own, got_z, own_t, total, sems):
    nz, ny, nx = dims
    k = panel.shape[0]

    z = lax.axis_index("rowa")
    b = lax.axis_index("rowb")
    c = lax.rem(b, CORES)
    x = lax.rem(b // CORES, nx)
    y = b // (CORES * nx)

    def device(zz, yy, xx, cc):
        return (zz, (yy * nx + xx) * CORES + cc)

    def ring_pairs(i, n):
        low = lax.rem(i, 2)
        return (lax.rem((i + 1) // 2, 2), i + 1 - 2 * low), (i // 2, n - 1 - i)

    def line_pairs(i, n):
        low = lax.rem(i, 2)
        return (low, i + 1 - 2 * low), (low, lax.rem(i - 1 + 2 * low + n, n))

    z_low, z_at = lax.rem(z, 2), z // 2
    pair_x, pair_y, pair_z = ring_pairs(x, nx), ring_pairs(y, ny), line_pairs(z, nz)
    pair_z2 = tuple((bit, 2 * at + z_low) for bit, at in line_pairs(z_at, nz // 2))

    def pick(pair, family):
        return tuple(a + family * (e - a) for a, e in zip(*pair))

    families = [lax.rem(s + c, 2) for s in range(2)]
    groups = [
        (
            [pick(pair, f) for pair in (pair_x, pair_y, pair_z)],
            [pick(pair_x, 1 - f), pick(pair_y, 1 - f), pick(pair_z2, f)],
        )
        for f in families
    ]

    def peer(s, step, mask):
        px, py, pz = groups[s][step]
        return device(pz[1] if mask & 4 else z, py[1] if mask & 2 else y, px[1] if mask & 1 else x, c)

    def index(s, step, mask):
        return sum(flip(bit, mask >> i & 1) * (1 << i) for i, (bit, _) in enumerate(groups[s][step]))

    other = device(z, y, x, 1 - c)
    far = [device(lax.rem(z + q * (nz // FAR), nz), y, x, c) for q in range(1, FAR)]

    barrier = pltpu.get_barrier_semaphore()
    everyone = far + [other] + [peer(s, 0, m) for s in range(2) for m in range(1, 8)]
    everyone += [peer(s, 1, m) for s in range(2) for m in range(4, 8)]
    for device_id in everyone:
        pl.semaphore_signal(barrier, inc=1, device_id=device_id, device_id_type=MESH)

    used, sent, started = [0], [], {}

    def start(key, src, dst, device_id):
        at = used[0]
        used[0] += 2
        cp = started[key] = pltpu.make_async_remote_copy(
            src_ref=src, dst_ref=dst, send_sem=sems.at[at], recv_sem=sems.at[at + 1],
            device_id=device_id, device_id_type=MESH,
        )
        cp.start()
        sent.append(cp)

    def rows(off, count):
        return pl.ds(off if isinstance(off, int) else pl.multiple_of(off, 8), count)

    for cc in range(CORES):
        at = 0
        for job in JOBS[cc]:
            j0, j1 = job[-2:]
            if job[0] == "g":
                left, step = slab[:, job[1] * LANE : (job[1] + 1) * LANE].T, LANE
            else:
                left, step = panel[...], k
            v = dot(left, slab[:, j0 * LANE : j1 * LANE])
            for j in range(j1 - j0):
                part[cc, at : at + step, :] = v[:, j * LANE : (j + 1) * LANE]
                at += step

    pl.semaphore_wait(barrier, len(everyone))

    streams = range(2)
    off_1 = [FIRST[s] + index(s, 0, 0) * PIECE[s] for s in streams]
    off_2 = [off_1[s] + index(s, 1, 0) * LAST[s] for s in streams]

    for s in streams:
        where = pl.ds(FIRST[s], SIZES[s])
        start(("c", s), part.at[1 - c, where], got_c.at[where], other)
    for s in streams:
        started["c", s].wait_recv()
        where = pl.ds(FIRST[s], SIZES[s])
        got_c[where, :] = part[c, where, :] + got_c[where, :]
        for m in range(1, 8):
            src = got_c.at[rows(FIRST[s] + index(s, 0, m) * PIECE[s], PIECE[s])]
            start((1, s, m), src, got_1.at[m - 1, pl.ds(FIRST[s] // 8, PIECE[s])], peer(s, 0, m))
    for s in streams:
        v = got_c[rows(off_1[s], PIECE[s]), :]
        for m in range(1, 8):
            started[1, s, m].wait_recv()
            v = v + got_1[m - 1, FIRST[s] // 8 : FIRST[s] // 8 + PIECE[s], :]
        got_c[rows(off_1[s], PIECE[s]), :] = v
        for m in range(1, 8):
            src = got_c.at[rows(off_1[s] + index(s, 1, m) * LAST[s], LAST[s])]
            start((2, s, m), src, got_2.at[m - 1, pl.ds(LAST_AT[s], LAST[s])], peer(s, 1, m))
    for s in streams:
        v = got_c[rows(off_2[s], LAST[s]), :]
        for m in range(1, 8):
            started[2, s, m].wait_recv()
            v = v + got_2[m - 1, LAST_AT[s] : LAST_AT[s] + LAST[s], :]
        own[LAST_AT[s] : LAST_AT[s] + LAST[s], :] = v

    me_far = z // (nz // FAR)
    send_z, recv_z = used[0], used[0] + FAR - 1
    used[0] += 2 * FAR - 1

    def far_copy(q, slot):
        return pltpu.make_async_remote_copy(
            src_ref=own, dst_ref=got_z.at[slot], send_sem=sems.at[send_z + q - 1], recv_sem=sems.at[recv_z + slot],
            device_id=far[q - 1], device_id_type=MESH,
        )

    for q in range(1, FAR):
        cp = far_copy(q, me_far)
        cp.start()
        sent.append(cp)
    got_z[me_far] = own[...]
    for q in range(1, FAR):
        far_copy(q, lax.rem(me_far + q, FAR)).wait_recv()
    v = got_z[0]
    for q in range(1, FAR):
        v = v + got_z[q]
    own_t[...] = v

    for s in streams:
        where = rows(off_2[s], LAST[s])
        for m in range(1, 8):
            start((3, s, m), own_t.at[pl.ds(LAST_AT[s], LAST[s])], total.at[c, where], peer(s, 1, m))
        total[c, where, :] = own_t[LAST_AT[s] : LAST_AT[s] + LAST[s], :]
    for s in streams:
        for m in range(1, 8):
            started[3, s, m].wait_recv()
        where = total.at[c, rows(off_1[s], PIECE[s])]
        for m in range(1, 8):
            start((4, s, m), where, where, peer(s, 0, m))
    for s in streams:
        for m in range(1, 8):
            started[4, s, m].wait_recv()
        where = total.at[c, pl.ds(FIRST[s], SIZES[s])]
        start((5, s), where, where, other)

    def whole(half):
        for cc in range(CORES):
            @pl.when(half == cc)
            def _():
                for kind, i, j, at in places(cc, k):
                    if kind == "p":
                        first[:, j * LANE : (j + 1) * LANE] = total[cc, at : at + k, :]
                        continue
                    v = total[cc, at : at + LANE, :]
                    for a, e, w in ((i, j, v), (j, i, v.T))[: 2 if j > i else 1]:
                        high, low = split(w)
                        g_high[a * LANE : (a + 1) * LANE, e * LANE : (e + 1) * LANE] = high
                        g_low[a * LANE : (a + 1) * LANE, e * LANE : (e + 1) * LANE] = low

    whole(c)
    for s in streams:
        started[5, s].wait_recv()
    whole(1 - c)
    for cp in sent:
        cp.wait_send()


def passes_kernel(scale, slab, g_high, g_low, first, basis_ref, factor_ref, w_high, w_low, p_pad):
    k, d = first.shape
    w_high[0:k, :] = jnp.zeros((k, d), BF16)
    w_low[0:k, :] = jnp.zeros((k, d), BF16)
    p_pad[k : 2 * k, :] = jnp.zeros((k, d), BF16)
    current = first[...]
    row = lax.broadcasted_iota(jnp.int32, (k, 2 * k), 0)
    col = lax.broadcasted_iota(jnp.int32, (k, 2 * k), 1)
    eye = jnp.where(col == row + k, 1.0, 0.0)
    for step in range(ITERS):
        pb = current.astype(BF16)
        p_pad[0:k, :] = pb
        wh, wl = split(dot(pb, g_high[...]) + dot(pb, g_low[...]))
        if step == ITERS - 1:
            rows = slab.shape[0]
            ih, il = split(dot_t(pb, slab[...]))
        m = factor_rows(dot_t(wh, p_pad[...]) + dot_t(wl, p_pad[...]) + eye, k)
        mh, ml = split(m)
        if step < ITERS - 1:
            w_high[k : 2 * k, :] = wh
            w_low[k : 2 * k, :] = wl
            current = dot(mh, w_high[...]) + (dot(mh, w_low[...]) + dot(ml, w_high[...]))
        else:
            w_high[k : 2 * k, 0:rows] = ih
            w_low[k : 2 * k, 0:rows] = il
            ih, il = w_high[:, 0:rows], w_low[:, 0:rows]
            basis_ref[...] = (dot(mh, ih) + (dot(mh, il) + dot(ml, ih))) * scale
            factor_ref[...] = jnp.where(col >= row, m, 0.0)[:, 0:k] * (1.0 / scale)


def body(sizes, slab, panel):
    nz, ny, nx = sizes
    rows, d = slab.shape
    k = panel.shape[0]
    scale = math.sqrt(rows * nz * ny * nx * CORES)
    n_sems = 2 * (4 + 4 * 14) + 2 * FAR - 1
    params = functools.partial(pltpu.CompilerParams, vmem_limit_bytes=36 * 1024 * 1024)
    vmem = pl.BlockSpec(memory_space=pltpu.VMEM)

    g_high, g_low, first = pl.pallas_call(
        functools.partial(reduce_kernel, (nz, ny, nx)),
        out_shape=(
            jax.ShapeDtypeStruct((d, d), BF16), jax.ShapeDtypeStruct((d, d), BF16), jax.ShapeDtypeStruct((k, d), F32)
        ),
        in_specs=[vmem] * 2,
        out_specs=(vmem,) * 3,
        scratch_shapes=[
            pltpu.VMEM((CORES, HALF, LANE), F32),
            pltpu.VMEM((HALF, LANE), F32),
            pltpu.VMEM((7, HALF // 8, LANE), F32),
            pltpu.VMEM((7, OWN, LANE), F32),
            pltpu.VMEM((OWN, LANE), F32),
            pltpu.VMEM((FAR, OWN, LANE), F32),
            pltpu.VMEM((OWN, LANE), F32),
            pltpu.VMEM((CORES, HALF, LANE), F32),
            pltpu.SemaphoreType.DMA((n_sems,)),
        ],
        compiler_params=params(collective_id=0, has_side_effects=True),
        cost_estimate=pl.CostEstimate(flops=10**9, bytes_accessed=10**7, transcendentals=0),
    )(slab, panel)
    return pl.pallas_call(
        functools.partial(passes_kernel, scale),
        out_shape=(jax.ShapeDtypeStruct((k, rows), F32), jax.ShapeDtypeStruct((k, k), F32)),
        in_specs=[vmem] * 4,
        out_specs=(vmem,) * 2,
        scratch_shapes=[
            pltpu.VMEM((2 * k, d), BF16),
            pltpu.VMEM((2 * k, d), BF16),
            pltpu.VMEM((2 * k, d), BF16),
        ],
        compiler_params=params(),
        cost_estimate=pl.CostEstimate(flops=2 * 10**9, bytes_accessed=3 * 10**6, transcendentals=0),
    )(slab, g_high, g_low, first)


def solution(mesh):
    nz = mesh.shape["rowa"]
    side = math.isqrt(mesh.shape["rowb"] // CORES)
    in_specs = (P(("rowa", "rowb"), None), P(None, ("rowa", "rowb")))
    out_specs = (P(None, ("rowa", "rowb")), P())
    return jax.shard_map(
        functools.partial(body, (nz, side, side)),
        mesh=mesh, in_specs=in_specs, out_specs=out_specs, check_vma=False,
    )
```

```python
import functools
import math

import jax
import jax.numpy as jnp
from jax import lax
from jax.experimental import pallas as pl
from jax.experimental.pallas import tpu as pltpu
from jax.sharding import PartitionSpec as P

ITERS = 3
MESH = pl.DeviceIdType.MESH
F32 = jnp.float32
BF16 = jnp.bfloat16
LANE = 128
CORES = 2
PANEL = 8


def dot(a, b):
    return jnp.dot(a, b, preferred_element_type=F32)


def dot_t(a, b):
    return lax.dot_general(a, b, (((1,), (1,)), ((), ())), preferred_element_type=F32)


def split(v):
    high = v.astype(BF16)
    return high, (v - high.astype(F32)).astype(BF16)


def factor_rows(m, k):
    groups = [m[8 * i : 8 * i + 8, :] for i in range(k // 8)]
    full = groups[0].shape
    done = [[None] * 8 for _ in groups]
    for first in range(0, k, PANEL):
        g, s = divmod(first, 8)
        size = range(PANEL)
        rows = [jnp.broadcast_to(groups[g][s + q : s + q + 1, :], full) for q in size]
        cols = [
            {i: jnp.broadcast_to(groups[i][:, first + q : first + q + 1], full) for i in range(g + 1, len(groups))}
            for q in size
        ]
        piv = [[jnp.broadcast_to(rows[q][:, first + r : first + r + 1], full) for r in size] for q in size]
        inv = []
        for q in size:
            inv.append(pl.reciprocal(piv[q][q]))
            for r in range(q + 1, PANEL):
                t = piv[q][r] * inv[q]
                rows[r] = rows[r] - t * rows[q]
                for i in cols[r]:
                    cols[r][i] = cols[r][i] - t * cols[q][i]
                for w in range(r, PANEL):
                    piv[r][w] = piv[r][w] - t * piv[q][w]
            done[g][s + q] = rows[q] * lax.rsqrt(piv[q][q])
        scaled = [rows[q] * inv[q] for q in size]
        for i in range(g + 1, len(groups)):
            for q in size:
                groups[i] = groups[i] - cols[q][i] * scaled[q]
    sub = lax.broadcasted_iota(jnp.int32, full, 0)
    out = []
    for rows in done:
        v = rows[0]
        for q in range(1, 8):
            v = jnp.where(sub == q, rows[q], v)
        out.append(v)
    return jnp.concatenate(out, axis=0)


JOBS = ((("g", 0, 8), ("g", 6, 8), ("p", 0, 4)), (("g", 2, 8), ("g", 4, 8), ("p", 4, 8)))
SIZES = (12 * LANE, 8 * LANE)
FIRST = (0, SIZES[0])
HALF = sum(SIZES)
PIECE = tuple(size // 8 for size in SIZES)
LAST = tuple(size // 64 for size in SIZES)
LAST_AT = (0, LAST[0])
OWN = sum(LAST)
FAR = 4


def places(cc, k):
    at, out = 0, []
    for kind, lo, hi in JOBS[cc]:
        for i in (lo, lo + 1) if kind == "g" else (0,):
            for j in range(max(lo, i), hi):
                out.append((kind, i, j, at))
                at += LANE if kind == "g" else k
    return out


def flip(bit, mask):
    return bit + mask - 2 * bit * mask


def reduce_kernel(dims, slab, panel, g_high, g_low, first, part, got_c, got_1, got_2, own, got_z, own_t, total, sems):
    nz, ny, nx = dims
    k = panel.shape[0]

    z = lax.axis_index("rowa")
    b = lax.axis_index("rowb")
    c = lax.rem(b, CORES)
    x = lax.rem(b // CORES, nx)
    y = b // (CORES * nx)

    def device(zz, yy, xx, cc):
        return (zz, (yy * nx + xx) * CORES + cc)

    def ring_pairs(i, n):
        low = lax.rem(i, 2)
        return (lax.rem((i + 1) // 2, 2), i + 1 - 2 * low), (i // 2, n - 1 - i)

    def line_pairs(i, n):
        low = lax.rem(i, 2)
        return (low, i + 1 - 2 * low), (low, lax.rem(i - 1 + 2 * low + n, n))

    z_low, z_at = lax.rem(z, 2), z // 2
    pair_x, pair_y, pair_z = ring_pairs(x, nx), ring_pairs(y, ny), line_pairs(z, nz)
    pair_z2 = tuple((bit, 2 * at + z_low) for bit, at in line_pairs(z_at, nz // 2))

    def pick(pair, family):
        return tuple(a + family * (e - a) for a, e in zip(*pair))

    families = [lax.rem(s + c, 2) for s in range(2)]
    groups = [
        (
            [pick(pair, f) for pair in (pair_x, pair_y, pair_z)],
            [pick(pair_x, 1 - f), pick(pair_y, 1 - f), pick(pair_z2, f)],
        )
        for f in families
    ]

    def peer(s, step, mask):
        px, py, pz = groups[s][step]
        return device(pz[1] if mask & 4 else z, py[1] if mask & 2 else y, px[1] if mask & 1 else x, c)

    def index(s, step, mask):
        return sum(flip(bit, mask >> i & 1) * (1 << i) for i, (bit, _) in enumerate(groups[s][step]))

    other = device(z, y, x, 1 - c)
    far = [device(lax.rem(z + q * (nz // FAR), nz), y, x, c) for q in range(1, FAR)]

    barrier = pltpu.get_barrier_semaphore()
    everyone = far + [other] + [peer(s, 0, m) for s in range(2) for m in range(1, 8)]
    everyone += [peer(s, 1, m) for s in range(2) for m in range(4, 8)]
    for device_id in everyone:
        pl.semaphore_signal(barrier, inc=1, device_id=device_id, device_id_type=MESH)

    used, sent, started = [0], [], {}

    def start(key, src, dst, device_id):
        at = used[0]
        used[0] += 2
        cp = started[key] = pltpu.make_async_remote_copy(
            src_ref=src, dst_ref=dst, send_sem=sems.at[at], recv_sem=sems.at[at + 1],
            device_id=device_id, device_id_type=MESH,
        )
        cp.start()
        sent.append(cp)

    def drain(count):
        for cp in sent[:count]:
            cp.wait_send()
        del sent[:count]

    def rows(off, count):
        return pl.ds(off if isinstance(off, int) else pl.multiple_of(off, 8), count)

    def work(half):
        for cc in range(CORES):
            @pl.when(half == cc)
            def _():
                at = 0
                for kind, lo, hi in JOBS[cc]:
                    if kind == "g":
                        v = dot(slab[:, lo * LANE : (lo + 2) * LANE].T, slab[:, lo * LANE : hi * LANE])
                    else:
                        v = dot(panel[...], slab[:, lo * LANE : hi * LANE])
                    for i in (0, 1) if kind == "g" else (0,):
                        step = LANE if kind == "g" else k
                        for j in range(i, hi - lo):
                            part[cc, at : at + step, :] = v[i * step : (i + 1) * step, j * LANE : (j + 1) * LANE]
                            at += step

    work(1 - c)
    pl.semaphore_wait(barrier, len(everyone))

    streams = range(2)
    off_1 = [FIRST[s] + index(s, 0, 0) * PIECE[s] for s in streams]
    off_2 = [off_1[s] + index(s, 1, 0) * LAST[s] for s in streams]

    for s in streams:
        where = pl.ds(FIRST[s], SIZES[s])
        start(("c", s), part.at[1 - c, where], got_c.at[where], other)
    work(c)
    for s in streams:
        started["c", s].wait_recv()
        where = pl.ds(FIRST[s], SIZES[s])
        got_c[where, :] = part[c, where, :] + got_c[where, :]
        for m in range(7, 0, -1):
            src = got_c.at[rows(FIRST[s] + index(s, 0, m) * PIECE[s], PIECE[s])]
            start((1, s, m), src, got_1.at[m - 1, pl.ds(FIRST[s] // 8, PIECE[s])], peer(s, 0, m))
    for s in streams:
        v = got_c[rows(off_1[s], PIECE[s]), :]
        for m in range(1, 8):
            started[1, s, m].wait_recv()
            v = v + got_1[m - 1, FIRST[s] // 8 : FIRST[s] // 8 + PIECE[s], :]
        got_c[rows(off_1[s], PIECE[s]), :] = v
        for m in range(7, 0, -1):
            src = got_c.at[rows(off_1[s] + index(s, 1, m) * LAST[s], LAST[s])]
            start((2, s, m), src, got_2.at[m - 1, pl.ds(LAST_AT[s], LAST[s])], peer(s, 1, m))
    for s in streams:
        v = got_c[rows(off_2[s], LAST[s]), :]
        for m in range(1, 8):
            started[2, s, m].wait_recv()
            v = v + got_2[m - 1, LAST_AT[s] : LAST_AT[s] + LAST[s], :]
        own[LAST_AT[s] : LAST_AT[s] + LAST[s], :] = v

    me_far = z // (nz // FAR)
    send_z, recv_z = used[0], used[0] + FAR - 1
    used[0] += 2 * FAR - 1

    def far_copy(q, slot):
        return pltpu.make_async_remote_copy(
            src_ref=own, dst_ref=got_z.at[slot], send_sem=sems.at[send_z + q - 1], recv_sem=sems.at[recv_z + slot],
            device_id=far[q - 1], device_id_type=MESH,
        )

    for q in (2, 1, 3):
        far_copy(q, me_far).start()
    got_z[me_far] = own[...]
    drain(len(sent))
    for q in range(1, FAR):
        sent.append(far_copy(q, me_far))
    for q in range(1, FAR):
        far_copy(q, lax.rem(me_far + q, FAR)).wait_recv()
    v = got_z[0]
    for q in range(1, FAR):
        v = v + got_z[q]
    own_t[...] = v

    for s in streams:
        where = rows(off_2[s], LAST[s])
        for m in range(7, 0, -1):
            start((3, s, m), own_t.at[pl.ds(LAST_AT[s], LAST[s])], total.at[c, where], peer(s, 1, m))
        total[c, where, :] = own_t[LAST_AT[s] : LAST_AT[s] + LAST[s], :]
    before = len(sent)
    for s in streams:
        for m in range(1, 8):
            started[3, s, m].wait_recv()
        where = total.at[c, rows(off_1[s], PIECE[s])]
        for m in range(7, 0, -1):
            start((4, s, m), where, where, peer(s, 0, m))
    drain(before)
    for s in streams:
        for part_at, masks in enumerate((range(1, 4), range(4, 8))):
            for m in masks:
                started[4, s, m].wait_recv()
            begin = FIRST[s] + flip(z_low, part_at) * 4 * PIECE[s]
            where = total.at[c, rows(begin, 4 * PIECE[s])]
            start((5, s, part_at), where, where, other)

    def whole(half):
        for cc in range(CORES):
            @pl.when(half == cc)
            def _():
                for kind, i, j, at in places(cc, k):
                    if kind == "p":
                        first[:, j * LANE : (j + 1) * LANE] = total[cc, at : at + k, :]
                        continue
                    v = total[cc, at : at + LANE, :]
                    for a, e, w in ((i, j, v), (j, i, v.T))[: 2 if j > i else 1]:
                        high, low = split(w)
                        g_high[a * LANE : (a + 1) * LANE, e * LANE : (e + 1) * LANE] = high
                        g_low[a * LANE : (a + 1) * LANE, e * LANE : (e + 1) * LANE] = low

    whole(c)
    drain(len(sent) - 4)
    for s in streams:
        for part_at in range(2):
            started[5, s, part_at].wait_recv()
    whole(1 - c)
    drain(len(sent))


def passes_kernel(scale, slab, g_high, g_low, first, basis_ref, factor_ref, w_high, w_low, p_pad):
    k, d = first.shape
    w_high[0:k, :] = jnp.zeros((k, d), BF16)
    w_low[0:k, :] = jnp.zeros((k, d), BF16)
    p_pad[k : 2 * k, :] = jnp.zeros((k, d), BF16)
    current = first[...]
    row = lax.broadcasted_iota(jnp.int32, (k, 2 * k), 0)
    col = lax.broadcasted_iota(jnp.int32, (k, 2 * k), 1)
    eye = jnp.where(col == row + k, 1.0, 0.0)
    for step in range(ITERS):
        pb = current.astype(BF16)
        p_pad[0:k, :] = pb
        wh, wl = split(dot(pb, g_high[...]) + dot(pb, g_low[...]))
        if step == ITERS - 1:
            rows = slab.shape[0]
            ih, il = split(dot_t(pb, slab[...]))
        m = factor_rows(dot_t(wh, p_pad[...]) + dot_t(wl, p_pad[...]) + eye, k)
        mh, ml = split(m)
        if step < ITERS - 1:
            w_high[k : 2 * k, :] = wh
            w_low[k : 2 * k, :] = wl
            current = dot(mh, w_high[...]) + (dot(mh, w_low[...]) + dot(ml, w_high[...]))
        else:
            w_high[k : 2 * k, 0:rows] = ih
            w_low[k : 2 * k, 0:rows] = il
            ih, il = w_high[:, 0:rows], w_low[:, 0:rows]
            basis_ref[...] = (dot(mh, ih) + (dot(mh, il) + dot(ml, ih))) * scale
            factor_ref[...] = jnp.where(col >= row, m, 0.0)[:, 0:k] * (1.0 / scale)


def body(sizes, slab, panel):
    nz, ny, nx = sizes
    rows, d = slab.shape
    k = panel.shape[0]
    scale = math.sqrt(rows * nz * ny * nx * CORES)
    n_sems = 2 * (6 + 4 * 14) + 2 * FAR - 1
    params = functools.partial(pltpu.CompilerParams, vmem_limit_bytes=36 * 1024 * 1024)
    vmem = pl.BlockSpec(memory_space=pltpu.VMEM)

    g_high, g_low, first = pl.pallas_call(
        functools.partial(reduce_kernel, (nz, ny, nx)),
        out_shape=(
            jax.ShapeDtypeStruct((d, d), BF16), jax.ShapeDtypeStruct((d, d), BF16), jax.ShapeDtypeStruct((k, d), F32)
        ),
        in_specs=[vmem] * 2,
        out_specs=(vmem,) * 3,
        scratch_shapes=[
            pltpu.VMEM((CORES, HALF, LANE), F32),
            pltpu.VMEM((HALF, LANE), F32),
            pltpu.VMEM((7, HALF // 8, LANE), F32),
            pltpu.VMEM((7, OWN, LANE), F32),
            pltpu.VMEM((OWN, LANE), F32),
            pltpu.VMEM((FAR, OWN, LANE), F32),
            pltpu.VMEM((OWN, LANE), F32),
            pltpu.VMEM((CORES, HALF, LANE), F32),
            pltpu.SemaphoreType.DMA((n_sems,)),
        ],
        compiler_params=params(collective_id=0, has_side_effects=True),
        cost_estimate=pl.CostEstimate(flops=10**9, bytes_accessed=10**7, transcendentals=0),
    )(slab, panel)
    return pl.pallas_call(
        functools.partial(passes_kernel, scale),
        out_shape=(jax.ShapeDtypeStruct((k, rows), F32), jax.ShapeDtypeStruct((k, k), F32)),
        in_specs=[vmem] * 4,
        out_specs=(vmem,) * 2,
        scratch_shapes=[
            pltpu.VMEM((2 * k, d), BF16),
            pltpu.VMEM((2 * k, d), BF16),
            pltpu.VMEM((2 * k, d), BF16),
        ],
        compiler_params=params(),
        cost_estimate=pl.CostEstimate(flops=2 * 10**9, bytes_accessed=3 * 10**6, transcendentals=0),
    )(slab, g_high, g_low, first)


def solution(mesh):
    nz = mesh.shape["rowa"]
    side = math.isqrt(mesh.shape["rowb"] // CORES)
    in_specs = (P(("rowa", "rowb"), None), P(None, ("rowa", "rowb")))
    out_specs = (P(None, ("rowa", "rowb")), P())
    return jax.shard_map(
        functools.partial(body, (nz, side, side)),
        mesh=mesh, in_specs=in_specs, out_specs=out_specs, check_vma=False,
    )
```

```python
import functools
import math

import jax
import jax.numpy as jnp
from jax import lax
from jax.experimental import pallas as pl
from jax.experimental.pallas import tpu as pltpu
from jax.sharding import PartitionSpec as P

ITERS = 3
MESH = pl.DeviceIdType.MESH
F32 = jnp.float32
BF16 = jnp.bfloat16
LANE = 128
CORES = 2
PANEL = 8


def dot(a, b):
    return jnp.dot(a, b, preferred_element_type=F32)


def dot_t(a, b):
    return lax.dot_general(a, b, (((1,), (1,)), ((), ())), preferred_element_type=F32)


def split(v):
    high = v.astype(BF16)
    return high, (v - high.astype(F32)).astype(BF16)


def factor_rows(m, k):
    groups = [m[8 * i : 8 * i + 8, :] for i in range(k // 8)]
    full = groups[0].shape
    done = [[None] * 8 for _ in groups]
    for first in range(0, k, PANEL):
        g, s = divmod(first, 8)
        size = range(PANEL)
        rows = [jnp.broadcast_to(groups[g][s + q : s + q + 1, :], full) for q in size]
        cols = [
            {i: jnp.broadcast_to(groups[i][:, first + q : first + q + 1], full) for i in range(g + 1, len(groups))}
            for q in size
        ]
        piv = [[jnp.broadcast_to(rows[q][:, first + r : first + r + 1], full) for r in size] for q in size]
        inv = []
        for q in size:
            inv.append(pl.reciprocal(piv[q][q]))
            for r in range(q + 1, PANEL):
                t = piv[q][r] * inv[q]
                rows[r] = rows[r] - t * rows[q]
                for i in cols[r]:
                    cols[r][i] = cols[r][i] - t * cols[q][i]
                for w in range(r, PANEL):
                    piv[r][w] = piv[r][w] - t * piv[q][w]
            done[g][s + q] = rows[q] * lax.rsqrt(piv[q][q])
        scaled = [rows[q] * inv[q] for q in size]
        for i in range(g + 1, len(groups)):
            for q in size:
                groups[i] = groups[i] - cols[q][i] * scaled[q]
    sub = lax.broadcasted_iota(jnp.int32, full, 0)
    out = []
    for rows in done:
        v = rows[0]
        for q in range(1, 8):
            v = jnp.where(sub == q, rows[q], v)
        out.append(v)
    return jnp.concatenate(out, axis=0)


JOBS = ((("g", 0, 8), ("g", 6, 8), ("p", 0, 4)), (("g", 2, 8), ("g", 4, 8), ("p", 4, 8)))
SIZES = (12 * LANE, 8 * LANE)
FIRST = (0, SIZES[0])
HALF = sum(SIZES)
PIECE = tuple(size // 8 for size in SIZES)
LAST = tuple(size // 64 for size in SIZES)
LAST_AT = (0, LAST[0])
OWN = sum(LAST)
FAR = 4


def places(cc, k):
    at, out = 0, []
    for kind, lo, hi in JOBS[cc]:
        for i in (lo, lo + 1) if kind == "g" else (0,):
            for j in range(max(lo, i), hi):
                out.append((kind, i, j, at))
                at += LANE if kind == "g" else k
    return out


def flip(bit, mask):
    return bit + mask - 2 * bit * mask


def reduce_kernel(dims, slab, panel, g_high, g_low, first, part, got_c, got_1a, got_1b,
                  got_2a, got_2b, own, got_z, own_t, total, sems):
    nz, ny, nx = dims
    k = panel.shape[0]
    got_1, got_2 = (got_1a, got_1b), (got_2a, got_2b)

    z = lax.axis_index("rowa")
    b = lax.axis_index("rowb")
    c = lax.rem(b, CORES)
    x = lax.rem(b // CORES, nx)
    y = b // (CORES * nx)

    def device(zz, yy, xx, cc):
        return (zz, (yy * nx + xx) * CORES + cc)

    def ring_pairs(i, n):
        low = lax.rem(i, 2)
        return (lax.rem((i + 1) // 2, 2), i + 1 - 2 * low), (i // 2, n - 1 - i)

    def line_pairs(i, n):
        low = lax.rem(i, 2)
        return (low, i + 1 - 2 * low), (low, lax.rem(i - 1 + 2 * low + n, n))

    z_low, z_at = lax.rem(z, 2), z // 2
    pair_x, pair_y, pair_z = ring_pairs(x, nx), ring_pairs(y, ny), line_pairs(z, nz)
    pair_z2 = tuple((bit, 2 * at + z_low) for bit, at in line_pairs(z_at, nz // 2))

    def pick(pair, family):
        return tuple(a + family * (e - a) for a, e in zip(*pair))

    families = [lax.rem(s + c, 2) for s in range(2)]
    groups = [
        (
            [pick(pair, f) for pair in (pair_x, pair_y, pair_z)],
            [pick(pair_x, 1 - f), pick(pair_y, 1 - f), pick(pair_z2, f)],
        )
        for f in families
    ]

    def peer(s, step, mask):
        px, py, pz = groups[s][step]
        return device(pz[1] if mask & 4 else z, py[1] if mask & 2 else y, px[1] if mask & 1 else x, c)

    def index(s, step, mask):
        return sum(flip(bit, mask >> i & 1) * (1 << i) for i, (bit, _) in enumerate(groups[s][step]))

    other = device(z, y, x, 1 - c)
    far = [device(lax.rem(z + q * (nz // FAR), nz), y, x, c) for q in range(1, FAR)]

    barrier = pltpu.get_barrier_semaphore()
    everyone = far + [other] + [peer(s, 0, m) for s in range(2) for m in range(1, 8)]
    everyone += [peer(s, 1, m) for s in range(2) for m in range(4, 8)]
    for device_id in everyone:
        pl.semaphore_signal(barrier, inc=1, device_id=device_id, device_id_type=MESH)

    used, sent, started = [0], [], {}

    def copy(src, dst, at, device_id):
        return pltpu.make_async_remote_copy(
            src_ref=src, dst_ref=dst, send_sem=sems.at[at], recv_sem=sems.at[at + 1],
            device_id=device_id, device_id_type=MESH,
        )

    def start(key, copies, everything):
        at = used[0]
        used[0] += 2
        for src, dst, device_id in copies:
            copy(src, dst, at, device_id).start()
        cp = started[key] = copy(everything, everything, at, other)
        sent.append(cp)

    def drain(count):
        for cp in sent[:count]:
            cp.wait_send()
        del sent[:count]

    def rows(off, count):
        return pl.ds(off if isinstance(off, int) else pl.multiple_of(off, 8), count)

    def work(half):
        for cc in range(CORES):
            @pl.when(half == cc)
            def _():
                at = 0
                for kind, lo, hi in JOBS[cc]:
                    if kind == "g":
                        v = dot(slab[:, lo * LANE : (lo + 2) * LANE].T, slab[:, lo * LANE : hi * LANE])
                    else:
                        v = dot(panel[...], slab[:, lo * LANE : hi * LANE])
                    for i in (0, 1) if kind == "g" else (0,):
                        step = LANE if kind == "g" else k
                        for j in range(i, hi - lo):
                            part[cc, at : at + step, :] = v[i * step : (i + 1) * step, j * LANE : (j + 1) * LANE]
                            at += step

    work(1 - c)
    pl.semaphore_wait(barrier, len(everyone))

    streams = range(2)
    off_1 = [FIRST[s] + index(s, 0, 0) * PIECE[s] for s in streams]
    off_2 = [off_1[s] + index(s, 1, 0) * LAST[s] for s in streams]

    for s in streams:
        where = pl.ds(FIRST[s], SIZES[s])
        start(("c", s), [(part.at[1 - c, where], got_c.at[where], other)], got_c.at[where])
    work(c)
    for s in streams:
        started["c", s].wait_recv()
        where = pl.ds(FIRST[s], SIZES[s])
        got_c[where, :] = part[c, where, :] + got_c[where, :]
        copies = [
            (got_c.at[rows(FIRST[s] + index(s, 0, m) * PIECE[s], PIECE[s])], got_1[s].at[m - 1], peer(s, 0, m))
            for m in range(7, 0, -1)
        ]
        start((1, s), copies, got_1[s])
    for s in streams:
        started[1, s].wait_recv()
        v = got_c[rows(off_1[s], PIECE[s]), :]
        for m in range(1, 8):
            v = v + got_1[s][m - 1]
        got_c[rows(off_1[s], PIECE[s]), :] = v
        copies = [
            (got_c.at[rows(off_1[s] + index(s, 1, m) * LAST[s], LAST[s])], got_2[s].at[m - 1], peer(s, 1, m))
            for m in range(7, 0, -1)
        ]
        start((2, s), copies, got_2[s])
    for s in streams:
        started[2, s].wait_recv()
        v = got_c[rows(off_2[s], LAST[s]), :]
        for m in range(1, 8):
            v = v + got_2[s][m - 1]
        own[LAST_AT[s] : LAST_AT[s] + LAST[s], :] = v

    me_far = z // (nz // FAR)
    send_z, recv_z = used[0], used[0] + FAR - 1
    used[0] += 2 * FAR - 1

    def far_copy(q, slot):
        return pltpu.make_async_remote_copy(
            src_ref=own, dst_ref=got_z.at[slot], send_sem=sems.at[send_z + q - 1], recv_sem=sems.at[recv_z + slot],
            device_id=far[q - 1], device_id_type=MESH,
        )

    for q in (2, 1, 3):
        far_copy(q, me_far).start()
    got_z[me_far] = own[...]
    drain(len(sent))
    for q in range(1, FAR):
        sent.append(far_copy(q, me_far))
    for q in range(1, FAR):
        far_copy(q, lax.rem(me_far + q, FAR)).wait_recv()
    v = got_z[0]
    for q in range(1, FAR):
        v = v + got_z[q]
    own_t[...] = v

    for s in streams:
        where = rows(off_2[s], LAST[s])
        src = own_t.at[pl.ds(LAST_AT[s], LAST[s])]
        copies = [(src, total.at[c, where], peer(s, 1, m)) for m in range(7, 0, -1)]
        start((3, s), copies, total.at[c, pl.ds(FIRST[s], 7 * LAST[s])])
        total[c, where, :] = own_t[LAST_AT[s] : LAST_AT[s] + LAST[s], :]
    before = len(sent)
    for s in streams:
        started[3, s].wait_recv()
        where = total.at[c, rows(off_1[s], PIECE[s])]
        for part_at, masks in enumerate(((3, 2, 1), (7, 6, 5, 4))):
            copies = [(where, where, peer(s, 0, m)) for m in masks]
            start((4, s, part_at), copies, total.at[c, pl.ds(FIRST[s], len(masks) * PIECE[s])])
    drain(before)
    for s in streams:
        for part_at in range(2):
            started[4, s, part_at].wait_recv()
            begin = FIRST[s] + flip(z_low, part_at) * 4 * PIECE[s]
            where = total.at[c, rows(begin, 4 * PIECE[s])]
            start((5, s, part_at), [(where, where, other)], where)

    def whole(half, s):
        for cc in range(CORES):
            @pl.when(half == cc)
            def _():
                for kind, i, j, at in places(cc, k):
                    if (at >= SIZES[0]) != s:
                        continue
                    if kind == "p":
                        first[:, j * LANE : (j + 1) * LANE] = total[cc, at : at + k, :]
                        continue
                    v = total[cc, at : at + LANE, :]
                    for a, e, w in ((i, j, v), (j, i, v.T))[: 2 if j > i else 1]:
                        high, low = split(w)
                        g_high[a * LANE : (a + 1) * LANE, e * LANE : (e + 1) * LANE] = high
                        g_low[a * LANE : (a + 1) * LANE, e * LANE : (e + 1) * LANE] = low

    for s in streams:
        whole(c, s)
    drain(len(sent) - 4)
    for s in streams:
        for part_at in range(2):
            started[5, s, part_at].wait_recv()
        whole(1 - c, s)
    drain(len(sent))


def passes_kernel(scale, slab, g_high, g_low, first, basis_ref, factor_ref, w_high, w_low, w_both, p_pad):
    k, d = first.shape
    w_high[0:k, :] = jnp.zeros((k, d), BF16)
    w_low[0:k, :] = jnp.zeros((k, d), BF16)
    p_pad[k : 2 * k, :] = jnp.zeros((k, d), BF16)
    current = first[...]
    row = lax.broadcasted_iota(jnp.int32, (k, 2 * k), 0)
    col = lax.broadcasted_iota(jnp.int32, (k, 2 * k), 1)
    eye = jnp.where(col == row + k, 1.0, 0.0)
    for step in range(ITERS):
        pb = current.astype(BF16)
        p_pad[0:k, :] = pb
        wh, wl = split(dot(pb, g_high[...]) + dot(pb, g_low[...]))
        if step == ITERS - 1:
            rows = slab.shape[0]
            ih, il = split(dot_t(pb, slab[...]))
        w_both[0:k, :] = wh
        w_both[k : 2 * k, :] = wl
        gram = dot_t(w_both[...], p_pad[...])
        m = factor_rows(gram[0:k, :] + gram[k : 2 * k, :] + eye, k)
        mh, ml = split(m)
        if step < ITERS - 1:
            w_high[k : 2 * k, :] = wh
            w_low[k : 2 * k, :] = wl
            both = dot(jnp.concatenate([mh, ml], axis=0), w_high[...])
            current = both[0:k, :] + (dot(mh, w_low[...]) + both[k : 2 * k, :])
        else:
            w_high[k : 2 * k, 0:rows] = ih
            w_low[k : 2 * k, 0:rows] = il
            ih, il = w_high[:, 0:rows], w_low[:, 0:rows]
            basis_ref[...] = (dot(mh, ih) + (dot(mh, il) + dot(ml, ih))) * scale
            factor_ref[...] = jnp.where(col >= row, m, 0.0)[:, 0:k] * (1.0 / scale)


def body(sizes, slab, panel):
    nz, ny, nx = sizes
    rows, d = slab.shape
    k = panel.shape[0]
    scale = math.sqrt(rows * nz * ny * nx * CORES)
    n_sems = 2 * 16 + 2 * FAR - 1
    params = functools.partial(pltpu.CompilerParams, vmem_limit_bytes=36 * 1024 * 1024)
    vmem = pl.BlockSpec(memory_space=pltpu.VMEM)

    g_high, g_low, first = pl.pallas_call(
        functools.partial(reduce_kernel, (nz, ny, nx)),
        out_shape=(
            jax.ShapeDtypeStruct((d, d), BF16), jax.ShapeDtypeStruct((d, d), BF16), jax.ShapeDtypeStruct((k, d), F32)
        ),
        in_specs=[vmem] * 2,
        out_specs=(vmem,) * 3,
        scratch_shapes=[
            pltpu.VMEM((CORES, HALF, LANE), F32),
            pltpu.VMEM((HALF, LANE), F32),
            *[pltpu.VMEM((7, size, LANE), F32) for size in PIECE + LAST],
            pltpu.VMEM((OWN, LANE), F32),
            pltpu.VMEM((FAR, OWN, LANE), F32),
            pltpu.VMEM((OWN, LANE), F32),
            pltpu.VMEM((CORES, HALF, LANE), F32),
            pltpu.SemaphoreType.DMA((n_sems,)),
        ],
        compiler_params=params(collective_id=0, has_side_effects=True),
        cost_estimate=pl.CostEstimate(flops=10**9, bytes_accessed=10**7, transcendentals=0),
    )(slab, panel)
    return pl.pallas_call(
        functools.partial(passes_kernel, scale),
        out_shape=(jax.ShapeDtypeStruct((k, rows), F32), jax.ShapeDtypeStruct((k, k), F32)),
        in_specs=[vmem] * 4,
        out_specs=(vmem,) * 2,
        scratch_shapes=[
            pltpu.VMEM((2 * k, d), BF16),
            pltpu.VMEM((2 * k, d), BF16),
            pltpu.VMEM((2 * k, d), BF16),
            pltpu.VMEM((2 * k, d), BF16),
        ],
        compiler_params=params(),
        cost_estimate=pl.CostEstimate(flops=2 * 10**9, bytes_accessed=3 * 10**6, transcendentals=0),
    )(slab, g_high, g_low, first)


def solution(mesh):
    nz = mesh.shape["rowa"]
    side = math.isqrt(mesh.shape["rowb"] // CORES)
    in_specs = (P(("rowa", "rowb"), None), P(None, ("rowa", "rowb")))
    out_specs = (P(None, ("rowa", "rowb")), P())
    return jax.shard_map(
        functools.partial(body, (nz, side, side)),
        mesh=mesh, in_specs=in_specs, out_specs=out_specs, check_vma=False,
    )
```

```python
import functools
import math

import jax
import jax.numpy as jnp
from jax import lax
from jax.experimental import pallas as pl
from jax.experimental.pallas import tpu as pltpu
from jax.sharding import PartitionSpec as P

ITERS = 3
MESH = pl.DeviceIdType.MESH
F32 = jnp.float32
BF16 = jnp.bfloat16
LANE = 128
CORES = 2
PANEL = 8


def dot(a, b):
    return jnp.dot(a, b, preferred_element_type=F32)


def dot_t(a, b):
    return lax.dot_general(a, b, (((1,), (1,)), ((), ())), preferred_element_type=F32)


def split(v):
    high = v.astype(BF16)
    return high, (v - high.astype(F32)).astype(BF16)


def factor_rows(m, k):
    groups = [m[8 * i : 8 * i + 8, :] for i in range(k // 8)]
    full = groups[0].shape
    done = [[None] * 8 for _ in groups]
    for first in range(0, k, PANEL):
        g, s = divmod(first, 8)
        size = range(PANEL)
        rows = [jnp.broadcast_to(groups[g][s + q : s + q + 1, :], full) for q in size]
        cols = [
            {i: jnp.broadcast_to(groups[i][:, first + q : first + q + 1], full) for i in range(g + 1, len(groups))}
            for q in size
        ]
        piv = [[jnp.broadcast_to(rows[q][:, first + r : first + r + 1], full) for r in size] for q in size]
        inv = []
        for q in size:
            inv.append(pl.reciprocal(piv[q][q]))
            for r in range(q + 1, PANEL):
                t = piv[q][r] * inv[q]
                rows[r] = rows[r] - t * rows[q]
                for i in cols[r]:
                    cols[r][i] = cols[r][i] - t * cols[q][i]
                for w in range(r, PANEL):
                    piv[r][w] = piv[r][w] - t * piv[q][w]
            done[g][s + q] = rows[q] * lax.rsqrt(piv[q][q])
        scaled = [rows[q] * inv[q] for q in size]
        for i in range(g + 1, len(groups)):
            for q in size:
                groups[i] = groups[i] - cols[q][i] * scaled[q]
    sub = lax.broadcasted_iota(jnp.int32, full, 0)
    out = []
    for rows in done:
        v = rows[0]
        for q in range(1, 8):
            v = jnp.where(sub == q, rows[q], v)
        out.append(v)
    return jnp.concatenate(out, axis=0)


JOBS = ((("g", 0, 8), ("g", 6, 8), ("p", 0, 4)), (("g", 2, 8), ("p", 4, 8), ("g", 4, 8)))
EARLY = (1, 2)
SIZES = (12 * LANE, 8 * LANE)
FIRST = (0, SIZES[0])
HALF = sum(SIZES)
PIECE = tuple(size // 8 for size in SIZES)
LAST = tuple(size // 64 for size in SIZES)
LAST_AT = (0, LAST[0])
OWN = sum(LAST)
FAR = 4


def places(cc, k):
    at, out = 0, []
    for kind, lo, hi in JOBS[cc]:
        for i in (lo, lo + 1) if kind == "g" else (0,):
            for j in range(max(lo, i), hi):
                out.append((kind, i, j, at))
                at += LANE if kind == "g" else k
    return out


def flip(bit, mask):
    return bit + mask - 2 * bit * mask


def reduce_kernel(dims, slab, panel, g_high, g_low, first, part, got_c, got_1a, got_1b,
                  got_2a, got_2b, own, got_z, own_t, total, known, sems):
    nz, ny, nx = dims
    k = panel.shape[0]
    got_1, got_2 = (got_1a, got_1b), (got_2a, got_2b)

    z = lax.axis_index("rowa")
    b = lax.axis_index("rowb")
    c = lax.rem(b, CORES)
    x = lax.rem(b // CORES, nx)
    y = b // (CORES * nx)

    def device(zz, yy, xx, cc):
        return (zz, (yy * nx + xx) * CORES + cc)

    def ring_pairs(i, n):
        low = lax.rem(i, 2)
        return (lax.rem((i + 1) // 2, 2), i + 1 - 2 * low), (i // 2, n - 1 - i)

    def line_pairs(i, n):
        low = lax.rem(i, 2)
        return (low, i + 1 - 2 * low), (low, lax.rem(i - 1 + 2 * low + n, n))

    z_low, z_at = lax.rem(z, 2), z // 2
    pair_x, pair_y, pair_z = ring_pairs(x, nx), ring_pairs(y, ny), line_pairs(z, nz)
    pair_z2 = tuple((bit, 2 * at + z_low) for bit, at in line_pairs(z_at, nz // 2))

    def pick(pair, family):
        return tuple(a + family * (e - a) for a, e in zip(*pair))

    families = [lax.rem(s + c, 2) for s in range(2)]
    groups = [
        (
            [pick(pair, f) for pair in (pair_x, pair_y, pair_z)],
            [pick(pair_x, 1 - f), pick(pair_y, 1 - f), pick(pair_z2, f)],
        )
        for f in families
    ]

    def peer(s, step, mask):
        px, py, pz = groups[s][step]
        return device(pz[1] if mask & 4 else z, py[1] if mask & 2 else y, px[1] if mask & 1 else x, c)

    def index(s, step, mask):
        return sum(flip(bit, mask >> i & 1) * (1 << i) for i, (bit, _) in enumerate(groups[s][step]))

    other = device(z, y, x, 1 - c)
    far = [device(lax.rem(z + q * (nz // FAR), nz), y, x, c) for q in range(1, FAR)]

    barrier = pltpu.get_barrier_semaphore()
    everyone = [other] + [peer(s, 0, m) for s in range(2) for m in range(1, 8)]
    everyone += [peer(s, 1, m) for s in range(2) for m in range(4, 8)]
    for device_id in everyone:
        pl.semaphore_signal(barrier, inc=1, device_id=device_id, device_id_type=MESH)

    def tell(level, devices):
        for device_id in devices:
            pl.semaphore_signal(known.at[level], inc=1, device_id=device_id, device_id_type=MESH)

    used, sent, started = [0], [], {}

    def copy(src, dst, at, device_id):
        return pltpu.make_async_remote_copy(
            src_ref=src, dst_ref=dst, send_sem=sems.at[at], recv_sem=sems.at[at + 1],
            device_id=device_id, device_id_type=MESH,
        )

    def start(key, copies, everything):
        at = used[0]
        used[0] += 2
        for src, dst, device_id in copies:
            copy(src, dst, at, device_id).start()
        cp = started[key] = copy(everything, everything, at, other)
        sent.append(cp)

    def drain(count):
        for cp in sent[:count]:
            cp.wait_send()
        del sent[:count]

    def rows(off, count):
        return pl.ds(off if isinstance(off, int) else pl.multiple_of(off, 8), count)

    def work(half, stream):
        for cc in range(CORES):
            @pl.when(half == cc)
            def _():
                at = 0
                for number, (kind, lo, hi) in enumerate(JOBS[cc]):
                    mine = (number >= EARLY[cc]) == stream
                    if mine and kind == "g":
                        v = dot(slab[:, lo * LANE : (lo + 2) * LANE].T, slab[:, lo * LANE : hi * LANE])
                    elif mine:
                        v = dot(panel[...], slab[:, lo * LANE : hi * LANE])
                    for i in (0, 1) if kind == "g" else (0,):
                        step = LANE if kind == "g" else k
                        for j in range(i, hi - lo):
                            if mine:
                                part[cc, at : at + step, :] = v[i * step : (i + 1) * step, j * LANE : (j + 1) * LANE]
                            at += step

    streams = range(2)
    off_1 = [FIRST[s] + index(s, 0, 0) * PIECE[s] for s in streams]
    off_2 = [off_1[s] + index(s, 1, 0) * LAST[s] for s in streams]

    for s in streams:
        work(1 - c, s)
        if s == 0:
            pl.semaphore_wait(barrier, len(everyone))
        where = pl.ds(FIRST[s], SIZES[s])
        start(("c", s), [(part.at[1 - c, where], got_c.at[where], other)], got_c.at[where])
    tell(0, [peer(s, 1, 4) for s in streams])
    for s in streams:
        work(c, s)
        started["c", s].wait_recv()
        where = pl.ds(FIRST[s], SIZES[s])
        got_c[where, :] = part[c, where, :] + got_c[where, :]
        copies = [
            (got_c.at[rows(FIRST[s] + index(s, 0, m) * PIECE[s], PIECE[s])], got_1[s].at[m - 1], peer(s, 0, m))
            for m in range(7, 0, -1)
        ]
        start((1, s), copies, got_1[s])
    pl.semaphore_wait(known.at[0], 2)
    tell(1, [far[0], far[2]])
    for s in streams:
        started[1, s].wait_recv()
        v = got_c[rows(off_1[s], PIECE[s]), :]
        for m in range(1, 8):
            v = v + got_1[s][m - 1]
        got_c[rows(off_1[s], PIECE[s]), :] = v
        copies = [
            (got_c.at[rows(off_1[s] + index(s, 1, m) * LAST[s], LAST[s])], got_2[s].at[m - 1], peer(s, 1, m))
            for m in range(7, 0, -1)
        ]
        start((2, s), copies, got_2[s])
    for s in streams:
        started[2, s].wait_recv()
        v = got_c[rows(off_2[s], LAST[s]), :]
        for m in range(1, 8):
            v = v + got_2[s][m - 1]
        own[LAST_AT[s] : LAST_AT[s] + LAST[s], :] = v

    me_far = z // (nz // FAR)
    send_z, recv_z = used[0], used[0] + FAR - 1
    used[0] += 2 * FAR - 1

    def far_copy(q, slot):
        return pltpu.make_async_remote_copy(
            src_ref=own, dst_ref=got_z.at[slot], send_sem=sems.at[send_z + q - 1], recv_sem=sems.at[recv_z + slot],
            device_id=far[q - 1], device_id_type=MESH,
        )

    pl.semaphore_wait(known.at[1], 2)
    for q in (2, 1, 3):
        far_copy(q, me_far).start()
    got_z[me_far] = own[...]
    drain(len(sent))
    for q in range(1, FAR):
        sent.append(far_copy(q, me_far))
    for q in range(1, FAR):
        far_copy(q, lax.rem(me_far + q, FAR)).wait_recv()
    v = got_z[0]
    for q in range(1, FAR):
        v = v + got_z[q]
    own_t[...] = v

    for s in streams:
        where = rows(off_2[s], LAST[s])
        src = own_t.at[pl.ds(LAST_AT[s], LAST[s])]
        copies = [(src, total.at[c, where], peer(s, 1, m)) for m in range(7, 0, -1)]
        start((3, s), copies, total.at[c, pl.ds(FIRST[s], 7 * LAST[s])])
        total[c, where, :] = own_t[LAST_AT[s] : LAST_AT[s] + LAST[s], :]
    before = len(sent)
    for s in streams:
        started[3, s].wait_recv()
        where = total.at[c, rows(off_1[s], PIECE[s])]
        for part_at, masks in enumerate(((3, 2, 1), (7, 6, 5, 4))):
            copies = [(where, where, peer(s, 0, m)) for m in masks]
            start((4, s, part_at), copies, total.at[c, pl.ds(FIRST[s], len(masks) * PIECE[s])])
    drain(before)
    for s in streams:
        for part_at in range(2):
            started[4, s, part_at].wait_recv()
            begin = FIRST[s] + flip(z_low, part_at) * 4 * PIECE[s]
            where = total.at[c, rows(begin, 4 * PIECE[s])]
            start((5, s, part_at), [(where, where, other)], where)

    def whole(half, s):
        for cc in range(CORES):
            @pl.when(half == cc)
            def _():
                for kind, i, j, at in places(cc, k):
                    if (at >= SIZES[0]) != s:
                        continue
                    if kind == "p":
                        first[:, j * LANE : (j + 1) * LANE] = total[cc, at : at + k, :]
                        continue
                    v = total[cc, at : at + LANE, :]
                    for a, e, w in ((i, j, v), (j, i, v.T))[: 2 if j > i else 1]:
                        high, low = split(w)
                        g_high[a * LANE : (a + 1) * LANE, e * LANE : (e + 1) * LANE] = high
                        g_low[a * LANE : (a + 1) * LANE, e * LANE : (e + 1) * LANE] = low

    for s in streams:
        whole(c, s)
    drain(len(sent) - 4)
    for s in streams:
        for part_at in range(2):
            started[5, s, part_at].wait_recv()
        whole(1 - c, s)
    drain(len(sent))


def passes_kernel(scale, slab, g_high, g_low, first, basis_ref, factor_ref, w_high, w_low, w_both, p_pad):
    k, d = first.shape
    w_high[0:k, :] = jnp.zeros((k, d), BF16)
    w_low[0:k, :] = jnp.zeros((k, d), BF16)
    p_pad[k : 2 * k, :] = jnp.zeros((k, d), BF16)
    current = first[...]
    row = lax.broadcasted_iota(jnp.int32, (k, 2 * k), 0)
    col = lax.broadcasted_iota(jnp.int32, (k, 2 * k), 1)
    eye = jnp.where(col == row + k, 1.0, 0.0)
    for step in range(ITERS):
        pb = current.astype(BF16)
        p_pad[0:k, :] = pb
        wh, wl = split(dot(pb, g_high[...]) + dot(pb, g_low[...]))
        if step == ITERS - 1:
            rows = slab.shape[0]
            ih, il = split(dot_t(pb, slab[...]))
        w_both[0:k, :] = wh
        w_both[k : 2 * k, :] = wl
        gram = dot_t(w_both[...], p_pad[...])
        m = factor_rows(gram[0:k, :] + gram[k : 2 * k, :] + eye, k)
        mh, ml = split(m)
        if step < ITERS - 1:
            w_high[k : 2 * k, :] = wh
            w_low[k : 2 * k, :] = wl
            both = dot(jnp.concatenate([mh, ml], axis=0), w_high[...])
            current = both[0:k, :] + (dot(mh, w_low[...]) + both[k : 2 * k, :])
        else:
            w_high[k : 2 * k, 0:rows] = ih
            w_low[k : 2 * k, 0:rows] = il
            ih, il = w_high[:, 0:rows], w_low[:, 0:rows]
            basis_ref[...] = (dot(mh, ih) + (dot(mh, il) + dot(ml, ih))) * scale
            factor_ref[...] = jnp.where(col >= row, m, 0.0)[:, 0:k] * (1.0 / scale)


def body(sizes, slab, panel):
    nz, ny, nx = sizes
    rows, d = slab.shape
    k = panel.shape[0]
    scale = math.sqrt(rows * nz * ny * nx * CORES)
    n_sems = 2 * 16 + 2 * FAR - 1
    params = functools.partial(pltpu.CompilerParams, vmem_limit_bytes=36 * 1024 * 1024)
    vmem = pl.BlockSpec(memory_space=pltpu.VMEM)

    g_high, g_low, first = pl.pallas_call(
        functools.partial(reduce_kernel, (nz, ny, nx)),
        out_shape=(
            jax.ShapeDtypeStruct((d, d), BF16), jax.ShapeDtypeStruct((d, d), BF16), jax.ShapeDtypeStruct((k, d), F32)
        ),
        in_specs=[vmem] * 2,
        out_specs=(vmem,) * 3,
        scratch_shapes=[
            pltpu.VMEM((CORES, HALF, LANE), F32),
            pltpu.VMEM((HALF, LANE), F32),
            *[pltpu.VMEM((7, size, LANE), F32) for size in PIECE + LAST],
            pltpu.VMEM((OWN, LANE), F32),
            pltpu.VMEM((FAR, OWN, LANE), F32),
            pltpu.VMEM((OWN, LANE), F32),
            pltpu.VMEM((CORES, HALF, LANE), F32),
            pltpu.SemaphoreType.REGULAR((2,)),
            pltpu.SemaphoreType.DMA((n_sems,)),
        ],
        compiler_params=params(collective_id=0, has_side_effects=True),
        cost_estimate=pl.CostEstimate(flops=10**9, bytes_accessed=10**7, transcendentals=0),
    )(slab, panel)
    return pl.pallas_call(
        functools.partial(passes_kernel, scale),
        out_shape=(jax.ShapeDtypeStruct((k, rows), F32), jax.ShapeDtypeStruct((k, k), F32)),
        in_specs=[vmem] * 4,
        out_specs=(vmem,) * 2,
        scratch_shapes=[
            pltpu.VMEM((2 * k, d), BF16),
            pltpu.VMEM((2 * k, d), BF16),
            pltpu.VMEM((2 * k, d), BF16),
            pltpu.VMEM((2 * k, d), BF16),
        ],
        compiler_params=params(),
        cost_estimate=pl.CostEstimate(flops=2 * 10**9, bytes_accessed=3 * 10**6, transcendentals=0),
    )(slab, g_high, g_low, first)


def solution(mesh):
    nz = mesh.shape["rowa"]
    side = math.isqrt(mesh.shape["rowb"] // CORES)
    in_specs = (P(("rowa", "rowb"), None), P(None, ("rowa", "rowb")))
    out_specs = (P(None, ("rowa", "rowb")), P())
    return jax.shard_map(
        functools.partial(body, (nz, side, side)),
        mesh=mesh, in_specs=in_specs, out_specs=out_specs, check_vma=False,
    )
```

```python
import functools
import math

import jax
import jax.numpy as jnp
from jax import lax
from jax.experimental import pallas as pl
from jax.experimental.pallas import tpu as pltpu
from jax.sharding import PartitionSpec as P

ITERS = 3
MESH = pl.DeviceIdType.MESH
F32 = jnp.float32
BF16 = jnp.bfloat16
LANE = 128
CORES = 2
PANEL = 8


def dot(a, b):
    return jnp.dot(a, b, preferred_element_type=F32)


def dot_t(a, b):
    return lax.dot_general(a, b, (((1,), (1,)), ((), ())), preferred_element_type=F32)


def split(v):
    high = v.astype(BF16)
    return high, (v - high.astype(F32)).astype(BF16)


def factor_rows(m, k):
    groups = [m[8 * i : 8 * i + 8, :] for i in range(k // 8)]
    full = groups[0].shape
    done = [[None] * 8 for _ in groups]
    for first in range(0, k, PANEL):
        g, s = divmod(first, 8)
        size = range(PANEL)
        rows = [jnp.broadcast_to(groups[g][s + q : s + q + 1, :], full) for q in size]
        cols = [
            {i: jnp.broadcast_to(groups[i][:, first + q : first + q + 1], full) for i in range(g + 1, len(groups))}
            for q in size
        ]
        piv = [[jnp.broadcast_to(rows[q][:, first + r : first + r + 1], full) for r in size] for q in size]
        inv = []
        for q in size:
            inv.append(pl.reciprocal(piv[q][q]))
            for r in range(q + 1, PANEL):
                t = piv[q][r] * inv[q]
                rows[r] = rows[r] - t * rows[q]
                for i in cols[r]:
                    cols[r][i] = cols[r][i] - t * cols[q][i]
                for w in range(r, PANEL):
                    piv[r][w] = piv[r][w] - t * piv[q][w]
            done[g][s + q] = rows[q] * lax.rsqrt(piv[q][q])
        scaled = [rows[q] * inv[q] for q in size]
        for i in range(g + 1, len(groups)):
            for q in size:
                groups[i] = groups[i] - cols[q][i] * scaled[q]
    sub = lax.broadcasted_iota(jnp.int32, full, 0)
    out = []
    for rows in done:
        v = rows[0]
        for q in range(1, 8):
            v = jnp.where(sub == q, rows[q], v)
        out.append(v)
    return jnp.concatenate(out, axis=0)


JOBS = ((("g", 0, 8), ("g", 6, 8), ("p", 0, 4)), (("g", 2, 8), ("p", 4, 8), ("g", 4, 8)))
EARLY = (1, 1)
ROWS = 20 * LANE
PIECE = ROWS // 8
OWN = PIECE // 8
FAR = 4


def places(cc, k):
    at, out = 0, []
    for kind, lo, hi in JOBS[cc]:
        for i in (lo, lo + 1) if kind == "g" else (0,):
            for j in range(max(lo, i), hi):
                out.append((kind, i, j, at))
                at += LANE if kind == "g" else k
    return out


def flip(bit, mask):
    return bit + mask - 2 * bit * mask


def reduce_kernel(dims, slab, panel, g_high, g_low, first, part, got_c, got_1, got_2, own, got_z, own_t, total, known, sems):
    nz, ny, nx = dims
    k = panel.shape[0]

    z = lax.axis_index("rowa")
    b = lax.axis_index("rowb")
    c = lax.rem(b, CORES)
    x = lax.rem(b // CORES, nx)
    y = b // (CORES * nx)

    def device(zz, yy, xx, cc):
        return (zz, (yy * nx + xx) * CORES + cc)

    def ring_pairs(i, n):
        low = lax.rem(i, 2)
        return (lax.rem((i + 1) // 2, 2), i + 1 - 2 * low), (i // 2, n - 1 - i)

    def line_pairs(i, n):
        low = lax.rem(i, 2)
        return (low, i + 1 - 2 * low), (low, lax.rem(i - 1 + 2 * low + n, n))

    z_low, z_at = lax.rem(z, 2), z // 2
    pair_x, pair_y, pair_z = ring_pairs(x, nx), ring_pairs(y, ny), line_pairs(z, nz)
    pair_z2 = tuple((bit, 2 * at + z_low) for bit, at in line_pairs(z_at, nz // 2))

    def pick(pair, family):
        return tuple(a + family * (e - a) for a, e in zip(*pair))

    groups = (
        [pick(pair, c) for pair in (pair_x, pair_y, pair_z)],
        [pick(pair_x, 1 - c), pick(pair_y, 1 - c), pick(pair_z2, c)],
    )
    others = (
        [pick(pair, 1 - c) for pair in (pair_x, pair_y, pair_z)],
        [pick(pair_x, c), pick(pair_y, c), pick(pair_z2, 1 - c)],
    )

    def member(group, mask):
        px, py, pz = group
        return device(pz[1] if mask & 4 else z, py[1] if mask & 2 else y, px[1] if mask & 1 else x, c)

    def peer(step, mask):
        return member(groups[step], mask)

    def index(step, mask):
        return sum(flip(bit, mask >> i & 1) * (1 << i) for i, (bit, _) in enumerate(groups[step]))

    other = device(z, y, x, 1 - c)
    far = [device(lax.rem(z + q * (nz // FAR), nz), y, x, c) for q in range(1, FAR)]

    barrier = pltpu.get_barrier_semaphore()
    near_z2 = [member(group[1], 4) for group in (groups, others)]
    everyone = [other] + [peer(0, m) for m in range(1, 8)] + [peer(1, m) for m in range(1, 8)] + near_z2[1:]
    for device_id in everyone:
        pl.semaphore_signal(barrier, inc=1, device_id=device_id, device_id_type=MESH)

    def tell(level, devices):
        for device_id in devices:
            pl.semaphore_signal(known.at[level], inc=1, device_id=device_id, device_id_type=MESH)

    used, sent, started = [0], [], {}

    def copy(src, dst, at, device_id):
        return pltpu.make_async_remote_copy(
            src_ref=src, dst_ref=dst, send_sem=sems.at[at], recv_sem=sems.at[at + 1],
            device_id=device_id, device_id_type=MESH,
        )

    def start(key, copies, everything):
        at = used[0]
        used[0] += 2
        for src, dst, device_id in copies:
            copy(src, dst, at, device_id).start()
        cp = started[key] = copy(everything, everything, at, other)
        sent.append(cp)

    def drain(count):
        for cp in sent[:count]:
            cp.wait_send()
        del sent[:count]

    def rows(off, count):
        return pl.ds(off if isinstance(off, int) else pl.multiple_of(off, 8), count)

    def work(half, later):
        for cc in range(CORES):
            @pl.when(half == cc)
            def _():
                at = 0
                for number, (kind, lo, hi) in enumerate(JOBS[cc]):
                    mine = (number >= EARLY[cc]) == later
                    if mine and kind == "g":
                        v = dot(slab[:, lo * LANE : (lo + 2) * LANE].T, slab[:, lo * LANE : hi * LANE])
                    elif mine:
                        v = dot(panel[...], slab[:, lo * LANE : hi * LANE])
                    for i in (0, 1) if kind == "g" else (0,):
                        step = LANE if kind == "g" else k
                        for j in range(i, hi - lo):
                            if mine:
                                part[cc, at : at + step, :] = v[i * step : (i + 1) * step, j * LANE : (j + 1) * LANE]
                            at += step

    off_1 = index(0, 0) * PIECE
    off_2 = off_1 + index(1, 0) * OWN
    halves = [pl.ds(h * ROWS // 2, ROWS // 2) for h in range(2)]

    for h in range(2):
        work(1 - c, h)
        if h == 0:
            pl.semaphore_wait(barrier, len(everyone))
        start(("c", h), [(part.at[1 - c, halves[h]], got_c.at[halves[h]], other)], got_c.at[halves[h]])
    tell(0, near_z2)
    at_1 = used[0]
    used[0] += 2
    for h in range(2):
        work(c, h)
        started["c", h].wait_recv()
        got_c[halves[h], :] = part[c, halves[h], :] + got_c[halves[h], :]
        cross = flip(z_low, h)
        z_to = z + cross * (groups[0][2][1] - z)
        for m in (3, 2, 1, 0):
            px, py, _ = groups[0]
            to = device(z_to, py[1] if m & 2 else y, px[1] if m & 1 else x, c)
            first_row = (flip(px[0], m & 1) + 2 * flip(py[0], m >> 1) + 4 * h) * PIECE
            slot = m - 1 + 4 * cross if m else 3
            send = copy(got_c.at[rows(first_row, PIECE)], got_1.at[slot], at_1, to)
            if m:
                send.start()
            else:
                pl.when(cross == 1)(send.start)
    started[1] = copy(got_1, got_1, at_1, other)
    sent.append(started[1])
    pl.semaphore_wait(known.at[0], 2)
    tell(1, [far[0], far[2]])
    started[1].wait_recv()
    v = got_c[rows(off_1, PIECE), :]
    for m in range(1, 8):
        v = v + got_1[m - 1]
    got_c[rows(off_1, PIECE), :] = v
    copies = [(got_c.at[rows(off_1 + index(1, m) * OWN, OWN)], got_2.at[m - 1], peer(1, m)) for m in range(7, 0, -1)]
    start(2, copies, got_2)
    started[2].wait_recv()
    v = got_c[rows(off_2, OWN), :]
    for m in range(1, 8):
        v = v + got_2[m - 1]
    own[...] = v

    me_far = z // (nz // FAR)
    send_z, recv_z = used[0], used[0] + FAR - 1
    used[0] += 2 * FAR - 1

    def far_copy(q, slot):
        return pltpu.make_async_remote_copy(
            src_ref=own, dst_ref=got_z.at[slot], send_sem=sems.at[send_z + q - 1], recv_sem=sems.at[recv_z + slot],
            device_id=far[q - 1], device_id_type=MESH,
        )

    pl.semaphore_wait(known.at[1], 2)
    for q in (2, 1, 3):
        far_copy(q, me_far).start()
    got_z[me_far] = own[...]
    drain(len(sent))
    for q in range(1, FAR):
        sent.append(far_copy(q, me_far))
    for q in range(1, FAR):
        far_copy(q, lax.rem(me_far + q, FAR)).wait_recv()
    v = got_z[0]
    for q in range(1, FAR):
        v = v + got_z[q]
    own_t[...] = v

    where = total.at[c, rows(off_2, OWN)]
    start(3, [(own_t, where, peer(1, m)) for m in range(7, 0, -1)], total.at[c, pl.ds(0, 7 * OWN)])
    total[c, rows(off_2, OWN), :] = own_t[...]
    before = len(sent)
    started[3].wait_recv()
    where = total.at[c, rows(off_1, PIECE)]
    for h, masks in enumerate(((3, 2, 1), (7, 6, 5, 4))):
        start((4, h), [(where, where, peer(0, m)) for m in masks], total.at[c, pl.ds(0, len(masks) * PIECE)])
    drain(before)
    for h in range(2):
        started[4, h].wait_recv()
        where = total.at[c, rows(flip(z_low, h) * (ROWS // 2), ROWS // 2)]
        start((5, h), [(where, where, other)], where)

    def whole(half, late):
        for cc in range(CORES):
            for h in range(2):
                @pl.when((half == cc) & (late == h))
                def _():
                    for kind, i, j, at in places(cc, k):
                        if (at >= ROWS // 2) != h:
                            continue
                        if kind == "p":
                            first[:, j * LANE : (j + 1) * LANE] = total[cc, at : at + k, :]
                            continue
                        v = total[cc, at : at + LANE, :]
                        for a, e, w in ((i, j, v), (j, i, v.T))[: 2 if j > i else 1]:
                            high, low = split(w)
                            g_high[a * LANE : (a + 1) * LANE, e * LANE : (e + 1) * LANE] = high
                            g_low[a * LANE : (a + 1) * LANE, e * LANE : (e + 1) * LANE] = low

    for h in range(2):
        whole(c, jnp.int32(h))
    drain(len(sent) - 2)
    for h in range(2):
        started[5, h].wait_recv()
        whole(1 - c, flip(z_low, h))
    drain(len(sent))


def passes_kernel(scale, slab, g_high, g_low, first, basis_ref, factor_ref, w_high, w_low, w_both, p_pad):
    k, d = first.shape
    w_high[0:k, :] = jnp.zeros((k, d), BF16)
    w_low[0:k, :] = jnp.zeros((k, d), BF16)
    p_pad[k : 2 * k, :] = jnp.zeros((k, d), BF16)
    current = first[...]
    row = lax.broadcasted_iota(jnp.int32, (k, 2 * k), 0)
    col = lax.broadcasted_iota(jnp.int32, (k, 2 * k), 1)
    eye = jnp.where(col == row + k, 1.0, 0.0)
    for step in range(ITERS):
        pb = current.astype(BF16)
        p_pad[0:k, :] = pb
        wh, wl = split(dot(pb, g_high[...]) + dot(pb, g_low[...]))
        if step == ITERS - 1:
            rows = slab.shape[0]
            ih, il = split(dot_t(pb, slab[...]))
        w_both[0:k, :] = wh
        w_both[k : 2 * k, :] = wl
        gram = dot_t(w_both[...], p_pad[...])
        m = factor_rows(gram[0:k, :] + gram[k : 2 * k, :] + eye, k)
        mh, ml = split(m)
        if step < ITERS - 1:
            w_high[k : 2 * k, :] = wh
            w_low[k : 2 * k, :] = wl
            both = dot(jnp.concatenate([mh, ml], axis=0), w_high[...])
            current = both[0:k, :] + (dot(mh, w_low[...]) + both[k : 2 * k, :])
        else:
            w_high[k : 2 * k, 0:rows] = ih
            w_low[k : 2 * k, 0:rows] = il
            ih, il = w_high[:, 0:rows], w_low[:, 0:rows]
            basis_ref[...] = (dot(mh, ih) + (dot(mh, il) + dot(ml, ih))) * scale
            factor_ref[...] = jnp.where(col >= row, m, 0.0)[:, 0:k] * (1.0 / scale)


def body(sizes, slab, panel):
    nz, ny, nx = sizes
    rows, d = slab.shape
    k = panel.shape[0]
    scale = math.sqrt(rows * nz * ny * nx * CORES)
    n_sems = 2 * 9 + 2 * FAR - 1
    params = functools.partial(pltpu.CompilerParams, vmem_limit_bytes=36 * 1024 * 1024)
    vmem = pl.BlockSpec(memory_space=pltpu.VMEM)

    g_high, g_low, first = pl.pallas_call(
        functools.partial(reduce_kernel, (nz, ny, nx)),
        out_shape=(
            jax.ShapeDtypeStruct((d, d), BF16), jax.ShapeDtypeStruct((d, d), BF16), jax.ShapeDtypeStruct((k, d), F32)
        ),
        in_specs=[vmem] * 2,
        out_specs=(vmem,) * 3,
        scratch_shapes=[
            pltpu.VMEM((CORES, ROWS, LANE), F32),
            pltpu.VMEM((ROWS, LANE), F32),
            pltpu.VMEM((7, PIECE, LANE), F32),
            pltpu.VMEM((7, OWN, LANE), F32),
            pltpu.VMEM((OWN, LANE), F32),
            pltpu.VMEM((FAR, OWN, LANE), F32),
            pltpu.VMEM((OWN, LANE), F32),
            pltpu.VMEM((CORES, ROWS, LANE), F32),
            pltpu.SemaphoreType.REGULAR((2,)),
            pltpu.SemaphoreType.DMA((n_sems,)),
        ],
        compiler_params=params(collective_id=0, has_side_effects=True),
        cost_estimate=pl.CostEstimate(flops=10**9, bytes_accessed=10**7, transcendentals=0),
    )(slab, panel)
    return pl.pallas_call(
        functools.partial(passes_kernel, scale),
        out_shape=(jax.ShapeDtypeStruct((k, rows), F32), jax.ShapeDtypeStruct((k, k), F32)),
        in_specs=[vmem] * 4,
        out_specs=(vmem,) * 2,
        scratch_shapes=[
            pltpu.VMEM((2 * k, d), BF16),
            pltpu.VMEM((2 * k, d), BF16),
            pltpu.VMEM((2 * k, d), BF16),
            pltpu.VMEM((2 * k, d), BF16),
        ],
        compiler_params=params(),
        cost_estimate=pl.CostEstimate(flops=2 * 10**9, bytes_accessed=3 * 10**6, transcendentals=0),
    )(slab, g_high, g_low, first)


def solution(mesh):
    nz = mesh.shape["rowa"]
    side = math.isqrt(mesh.shape["rowb"] // CORES)
    in_specs = (P(("rowa", "rowb"), None), P(None, ("rowa", "rowb")))
    out_specs = (P(None, ("rowa", "rowb")), P())
    return jax.shard_map(
        functools.partial(body, (nz, side, side)),
        mesh=mesh, in_specs=in_specs, out_specs=out_specs, check_vma=False,
    )
```

```python
import functools
import math

import jax
import jax.numpy as jnp
from jax import lax
from jax.experimental import pallas as pl
from jax.experimental.pallas import tpu as pltpu
from jax.sharding import PartitionSpec as P

ITERS = 3
MESH = pl.DeviceIdType.MESH
F32 = jnp.float32
BF16 = jnp.bfloat16
LANE = 128
CORES = 2
PANEL = 8


def dot(a, b):
    return jnp.dot(a, b, preferred_element_type=F32)


def dot_t(a, b):
    return lax.dot_general(a, b, (((1,), (1,)), ((), ())), preferred_element_type=F32)


def split(v):
    high = v.astype(BF16)
    return high, (v - high.astype(F32)).astype(BF16)


def factor_rows(m, k):
    groups = [m[8 * i : 8 * i + 8, :] for i in range(k // 8)]
    full = groups[0].shape
    done = [[None] * 8 for _ in groups]
    for first in range(0, k, PANEL):
        g, s = divmod(first, 8)
        size = range(PANEL)
        rows = [jnp.broadcast_to(groups[g][s + q : s + q + 1, :], full) for q in size]
        cols = [
            {i: jnp.broadcast_to(groups[i][:, first + q : first + q + 1], full) for i in range(g + 1, len(groups))}
            for q in size
        ]
        piv = [[jnp.broadcast_to(rows[q][:, first + r : first + r + 1], full) for r in size] for q in size]
        inv = []
        for q in size:
            inv.append(pl.reciprocal(piv[q][q]))
            for r in range(q + 1, PANEL):
                t = piv[q][r] * inv[q]
                rows[r] = rows[r] - t * rows[q]
                for i in cols[r]:
                    cols[r][i] = cols[r][i] - t * cols[q][i]
                for w in range(r, PANEL):
                    piv[r][w] = piv[r][w] - t * piv[q][w]
            done[g][s + q] = rows[q] * lax.rsqrt(piv[q][q])
        scaled = [rows[q] * inv[q] for q in size]
        for i in range(g + 1, len(groups)):
            for q in size:
                groups[i] = groups[i] - cols[q][i] * scaled[q]
    sub = lax.broadcasted_iota(jnp.int32, full, 0)
    out = []
    for rows in done:
        v = rows[0]
        for q in range(1, 8):
            v = jnp.where(sub == q, rows[q], v)
        out.append(v)
    return jnp.concatenate(out, axis=0)


JOBS = ((("g", 0, 8), ("g", 6, 8), ("p", 0, 4)), (("g", 2, 8), ("p", 4, 8), ("g", 4, 8)))
NEEDS = ((1, 1, 2, 3), (1, 2, 3, 3))
SIZES = (8 * LANE, 4 * LANE, 4 * LANE, 4 * LANE)
STREAMS = len(SIZES)
FIRST = tuple(sum(SIZES[:s]) for s in range(STREAMS))
HALF = sum(SIZES)
PIECE = tuple(size // 8 for size in SIZES)
LAST = tuple(size // 64 for size in SIZES)
LAST_AT = tuple(first // 64 for first in FIRST)
OWN = sum(LAST)
FAR = 4


def places(cc, k):
    at, out = 0, []
    for kind, lo, hi in JOBS[cc]:
        for i in (lo, lo + 1) if kind == "g" else (0,):
            for j in range(max(lo, i), hi):
                out.append((kind, i, j, at))
                at += LANE if kind == "g" else k
    return out


def flip(bit, mask):
    return bit + mask - 2 * bit * mask


def reduce_kernel(dims, slab, panel, g_high, g_low, first, part, got_c, own, got_z, own_t,
                  total, known, sems, *got):
    nz, ny, nx = dims
    k = panel.shape[0]
    got_1, got_2 = got[:STREAMS], got[STREAMS:]

    z = lax.axis_index("rowa")
    b = lax.axis_index("rowb")
    c = lax.rem(b, CORES)
    x = lax.rem(b // CORES, nx)
    y = b // (CORES * nx)

    def device(zz, yy, xx, cc):
        return (zz, (yy * nx + xx) * CORES + cc)

    def ring_pairs(i, n):
        low = lax.rem(i, 2)
        return (lax.rem((i + 1) // 2, 2), i + 1 - 2 * low), (i // 2, n - 1 - i)

    def line_pairs(i, n):
        low = lax.rem(i, 2)
        return (low, i + 1 - 2 * low), (low, lax.rem(i - 1 + 2 * low + n, n))

    z_low, z_at = lax.rem(z, 2), z // 2
    pair_x, pair_y, pair_z = ring_pairs(x, nx), ring_pairs(y, ny), line_pairs(z, nz)
    pair_z2 = tuple((bit, 2 * at + z_low) for bit, at in line_pairs(z_at, nz // 2))

    def pick(pair, family):
        return tuple(a + family * (e - a) for a, e in zip(*pair))

    families = [lax.rem(s + c, 2) for s in range(STREAMS)]
    groups = [
        (
            [pick(pair, f) for pair in (pair_x, pair_y, pair_z)],
            [pick(pair_x, 1 - f), pick(pair_y, 1 - f), pick(pair_z2, f)],
        )
        for f in families
    ]

    def peer(s, step, mask):
        px, py, pz = groups[s][step]
        return device(pz[1] if mask & 4 else z, py[1] if mask & 2 else y, px[1] if mask & 1 else x, c)

    def index(s, step, mask):
        return sum(flip(bit, mask >> i & 1) * (1 << i) for i, (bit, _) in enumerate(groups[s][step]))

    other = device(z, y, x, 1 - c)
    far = [device(lax.rem(z + q * (nz // FAR), nz), y, x, c) for q in range(1, FAR)]

    barrier = pltpu.get_barrier_semaphore()
    everyone = [other] + [peer(s, 0, m) for s in range(2) for m in range(1, 8)]
    everyone += [peer(s, 1, m) for s in range(2) for m in range(4, 8)]
    for device_id in everyone:
        pl.semaphore_signal(barrier, inc=1, device_id=device_id, device_id_type=MESH)

    def tell(level, devices):
        for device_id in devices:
            pl.semaphore_signal(known.at[level], inc=1, device_id=device_id, device_id_type=MESH)

    used, sent, started = [0], [], {}

    def copy(src, dst, at, device_id):
        return pltpu.make_async_remote_copy(
            src_ref=src, dst_ref=dst, send_sem=sems.at[at], recv_sem=sems.at[at + 1],
            device_id=device_id, device_id_type=MESH,
        )

    def start(key, copies, everything):
        at = used[0]
        used[0] += 2
        for src, dst, device_id in copies:
            copy(src, dst, at, device_id).start()
        cp = started[key] = copy(everything, everything, at, other)
        sent.append(cp)

    def drain(count):
        for cp in sent[:count]:
            cp.wait_send()
        del sent[:count]

    def rows(off, count):
        return pl.ds(off if isinstance(off, int) else pl.multiple_of(off, 8), count)

    def work(half, s):
        for cc in range(CORES):
            @pl.when(half == cc)
            def _():
                at = 0
                for number, (kind, lo, hi) in enumerate(JOBS[cc]):
                    mine = (NEEDS[cc][s - 1] if s else 0) <= number < NEEDS[cc][s]
                    if mine and kind == "g":
                        v = dot(slab[:, lo * LANE : (lo + 2) * LANE].T, slab[:, lo * LANE : hi * LANE])
                    elif mine:
                        v = dot(panel[...], slab[:, lo * LANE : hi * LANE])
                    for i in (0, 1) if kind == "g" else (0,):
                        step = LANE if kind == "g" else k
                        for j in range(i, hi - lo):
                            if mine:
                                part[cc, at : at + step, :] = v[i * step : (i + 1) * step, j * LANE : (j + 1) * LANE]
                            at += step

    streams = range(STREAMS)
    off_1 = [FIRST[s] + index(s, 0, 0) * PIECE[s] for s in streams]
    off_2 = [off_1[s] + index(s, 1, 0) * LAST[s] for s in streams]

    for s in streams:
        work(1 - c, s)
        if s == 0:
            pl.semaphore_wait(barrier, len(everyone))
        where = pl.ds(FIRST[s], SIZES[s])
        start(("c", s), [(part.at[1 - c, where], got_c.at[where], other)], got_c.at[where])
    tell(0, [peer(s, 1, 4) for s in range(2)])
    for s in streams:
        work(c, s)
        started["c", s].wait_recv()
        where = pl.ds(FIRST[s], SIZES[s])
        got_c[where, :] = part[c, where, :] + got_c[where, :]
        copies = [
            (got_c.at[rows(FIRST[s] + index(s, 0, m) * PIECE[s], PIECE[s])], got_1[s].at[m - 1], peer(s, 0, m))
            for m in range(7, 0, -1)
        ]
        start((1, s), copies, got_1[s])
    pl.semaphore_wait(known.at[0], 2)
    tell(1, [far[0], far[2]])
    for s in streams:
        started[1, s].wait_recv()
        v = got_c[rows(off_1[s], PIECE[s]), :]
        for m in range(1, 8):
            v = v + got_1[s][m - 1]
        got_c[rows(off_1[s], PIECE[s]), :] = v
        copies = [
            (got_c.at[rows(off_1[s] + index(s, 1, m) * LAST[s], LAST[s])], got_2[s].at[m - 1], peer(s, 1, m))
            for m in range(7, 0, -1)
        ]
        start((2, s), copies, got_2[s])
    for s in streams:
        started[2, s].wait_recv()
        v = got_c[rows(off_2[s], LAST[s]), :]
        for m in range(1, 8):
            v = v + got_2[s][m - 1]
        own[LAST_AT[s] : LAST_AT[s] + LAST[s], :] = v

    me_far = z // (nz // FAR)
    send_z, recv_z = used[0], used[0] + FAR - 1
    used[0] += 2 * FAR - 1

    def far_copy(q, slot):
        return pltpu.make_async_remote_copy(
            src_ref=own, dst_ref=got_z.at[slot], send_sem=sems.at[send_z + q - 1], recv_sem=sems.at[recv_z + slot],
            device_id=far[q - 1], device_id_type=MESH,
        )

    pl.semaphore_wait(known.at[1], 2)
    for q in (2, 1, 3):
        far_copy(q, me_far).start()
    got_z[me_far] = own[...]
    drain(len(sent))
    for q in range(1, FAR):
        sent.append(far_copy(q, me_far))
    for q in range(1, FAR):
        far_copy(q, lax.rem(me_far + q, FAR)).wait_recv()
    v = got_z[0]
    for q in range(1, FAR):
        v = v + got_z[q]
    own_t[...] = v

    for s in streams:
        where = rows(off_2[s], LAST[s])
        src = own_t.at[pl.ds(LAST_AT[s], LAST[s])]
        copies = [(src, total.at[c, where], peer(s, 1, m)) for m in range(7, 0, -1)]
        start((3, s), copies, total.at[c, pl.ds(FIRST[s], 7 * LAST[s])])
        total[c, where, :] = own_t[LAST_AT[s] : LAST_AT[s] + LAST[s], :]
    before = len(sent)
    for s in streams:
        started[3, s].wait_recv()
        where = total.at[c, rows(off_1[s], PIECE[s])]
        for part_at, masks in enumerate(((3, 2, 1), (7, 6, 5, 4))):
            copies = [(where, where, peer(s, 0, m)) for m in masks]
            start((4, s, part_at), copies, total.at[c, pl.ds(FIRST[s], len(masks) * PIECE[s])])
    drain(before)
    for s in streams:
        for part_at in range(2):
            started[4, s, part_at].wait_recv()
            begin = FIRST[s] + flip(z_low, part_at) * 4 * PIECE[s]
            where = total.at[c, rows(begin, 4 * PIECE[s])]
            start((5, s, part_at), [(where, where, other)], where)

    def whole(half, s):
        for cc in range(CORES):
            @pl.when(half == cc)
            def _():
                for kind, i, j, at in places(cc, k):
                    if not FIRST[s] <= at < FIRST[s] + SIZES[s]:
                        continue
                    if kind == "p":
                        first[:, j * LANE : (j + 1) * LANE] = total[cc, at : at + k, :]
                        continue
                    v = total[cc, at : at + LANE, :]
                    for a, e, w in ((i, j, v), (j, i, v.T))[: 2 if j > i else 1]:
                        high, low = split(w)
                        g_high[a * LANE : (a + 1) * LANE, e * LANE : (e + 1) * LANE] = high
                        g_low[a * LANE : (a + 1) * LANE, e * LANE : (e + 1) * LANE] = low

    for s in streams:
        whole(c, s)
    drain(len(sent) - 2 * STREAMS)
    for s in streams:
        for part_at in range(2):
            started[5, s, part_at].wait_recv()
        whole(1 - c, s)
    drain(len(sent))


def passes_kernel(scale, slab, g_high, g_low, first, basis_ref, factor_ref, w_high, w_low, w_both, p_pad):
    k, d = first.shape
    w_high[0:k, :] = jnp.zeros((k, d), BF16)
    w_low[0:k, :] = jnp.zeros((k, d), BF16)
    p_pad[k : 2 * k, :] = jnp.zeros((k, d), BF16)
    current = first[...]
    row = lax.broadcasted_iota(jnp.int32, (k, 2 * k), 0)
    col = lax.broadcasted_iota(jnp.int32, (k, 2 * k), 1)
    eye = jnp.where(col == row + k, 1.0, 0.0)
    for step in range(ITERS):
        pb = current.astype(BF16)
        p_pad[0:k, :] = pb
        wh, wl = split(dot(pb, g_high[...]) + dot(pb, g_low[...]))
        if step == ITERS - 1:
            rows = slab.shape[0]
            ih, il = split(dot_t(pb, slab[...]))
        w_both[0:k, :] = wh
        w_both[k : 2 * k, :] = wl
        gram = dot_t(w_both[...], p_pad[...])
        m = factor_rows(gram[0:k, :] + gram[k : 2 * k, :] + eye, k)
        mh, ml = split(m)
        if step < ITERS - 1:
            w_high[k : 2 * k, :] = wh
            w_low[k : 2 * k, :] = wl
            both = dot(jnp.concatenate([mh, ml], axis=0), w_high[...])
            current = both[0:k, :] + (dot(mh, w_low[...]) + both[k : 2 * k, :])
        else:
            w_high[k : 2 * k, 0:rows] = ih
            w_low[k : 2 * k, 0:rows] = il
            ih, il = w_high[:, 0:rows], w_low[:, 0:rows]
            basis_ref[...] = (dot(mh, ih) + (dot(mh, il) + dot(ml, ih))) * scale
            factor_ref[...] = jnp.where(col >= row, m, 0.0)[:, 0:k] * (1.0 / scale)


def body(sizes, slab, panel):
    nz, ny, nx = sizes
    rows, d = slab.shape
    k = panel.shape[0]
    scale = math.sqrt(rows * nz * ny * nx * CORES)
    n_sems = 2 * 8 * STREAMS + 2 * FAR - 1
    params = functools.partial(pltpu.CompilerParams, vmem_limit_bytes=36 * 1024 * 1024)
    vmem = pl.BlockSpec(memory_space=pltpu.VMEM)

    g_high, g_low, first = pl.pallas_call(
        functools.partial(reduce_kernel, (nz, ny, nx)),
        out_shape=(
            jax.ShapeDtypeStruct((d, d), BF16), jax.ShapeDtypeStruct((d, d), BF16), jax.ShapeDtypeStruct((k, d), F32)
        ),
        in_specs=[vmem] * 2,
        out_specs=(vmem,) * 3,
        scratch_shapes=[
            pltpu.VMEM((CORES, HALF, LANE), F32),
            pltpu.VMEM((HALF, LANE), F32),
            pltpu.VMEM((OWN, LANE), F32),
            pltpu.VMEM((FAR, OWN, LANE), F32),
            pltpu.VMEM((OWN, LANE), F32),
            pltpu.VMEM((CORES, HALF, LANE), F32),
            pltpu.SemaphoreType.REGULAR((2,)),
            pltpu.SemaphoreType.DMA((n_sems,)),
            *[pltpu.VMEM((7, size, LANE), F32) for size in PIECE + LAST],
        ],
        compiler_params=params(collective_id=0, has_side_effects=True),
        cost_estimate=pl.CostEstimate(flops=10**9, bytes_accessed=10**7, transcendentals=0),
    )(slab, panel)
    return pl.pallas_call(
        functools.partial(passes_kernel, scale),
        out_shape=(jax.ShapeDtypeStruct((k, rows), F32), jax.ShapeDtypeStruct((k, k), F32)),
        in_specs=[vmem] * 4,
        out_specs=(vmem,) * 2,
        scratch_shapes=[
            pltpu.VMEM((2 * k, d), BF16),
            pltpu.VMEM((2 * k, d), BF16),
            pltpu.VMEM((2 * k, d), BF16),
            pltpu.VMEM((2 * k, d), BF16),
        ],
        compiler_params=params(),
        cost_estimate=pl.CostEstimate(flops=2 * 10**9, bytes_accessed=3 * 10**6, transcendentals=0),
    )(slab, g_high, g_low, first)


def solution(mesh):
    nz = mesh.shape["rowa"]
    side = math.isqrt(mesh.shape["rowb"] // CORES)
    in_specs = (P(("rowa", "rowb"), None), P(None, ("rowa", "rowb")))
    out_specs = (P(None, ("rowa", "rowb")), P())
    return jax.shard_map(
        functools.partial(body, (nz, side, side)),
        mesh=mesh, in_specs=in_specs, out_specs=out_specs, check_vma=False,
    )
```

```python
import functools
import math

import jax
import jax.numpy as jnp
from jax import lax
from jax.experimental import pallas as pl
from jax.experimental.pallas import tpu as pltpu
from jax.sharding import PartitionSpec as P

ITERS = 3
MESH = pl.DeviceIdType.MESH
F32 = jnp.float32
BF16 = jnp.bfloat16
LANE = 128
CORES = 2
PANEL = 8


def dot(a, b):
    return jnp.dot(a, b, preferred_element_type=F32)


def dot_t(a, b):
    return lax.dot_general(a, b, (((1,), (1,)), ((), ())), preferred_element_type=F32)


def split(v):
    high = v.astype(BF16)
    return high, (v - high.astype(F32)).astype(BF16)


def factor_rows(m, k):
    groups = [m[8 * i : 8 * i + 8, :] for i in range(k // 8)]
    full = groups[0].shape
    done = [[None] * 8 for _ in groups]
    for first in range(0, k, PANEL):
        g, s = divmod(first, 8)
        size = range(PANEL)
        rows = [jnp.broadcast_to(groups[g][s + q : s + q + 1, :], full) for q in size]
        cols = [
            {i: jnp.broadcast_to(groups[i][:, first + q : first + q + 1], full) for i in range(g + 1, len(groups))}
            for q in size
        ]
        piv = [[jnp.broadcast_to(rows[q][:, first + r : first + r + 1], full) for r in size] for q in size]
        inv = []
        for q in size:
            inv.append(pl.reciprocal(piv[q][q]))
            for r in range(q + 1, PANEL):
                t = piv[q][r] * inv[q]
                rows[r] = rows[r] - t * rows[q]
                for i in cols[r]:
                    cols[r][i] = cols[r][i] - t * cols[q][i]
                for w in range(r, PANEL):
                    piv[r][w] = piv[r][w] - t * piv[q][w]
            done[g][s + q] = rows[q] * lax.rsqrt(piv[q][q])
        scaled = [rows[q] * inv[q] for q in size]
        for i in range(g + 1, len(groups)):
            for q in size:
                groups[i] = groups[i] - cols[q][i] * scaled[q]
    sub = lax.broadcasted_iota(jnp.int32, full, 0)
    out = []
    for rows in done:
        v = rows[0]
        for q in range(1, 8):
            v = jnp.where(sub == q, rows[q], v)
        out.append(v)
    return jnp.concatenate(out, axis=0)


JOBS = ((("g", 0, 8), ("g", 6, 8), ("p", 0, 4)), (("g", 2, 8), ("p", 4, 8), ("g", 4, 8)))
NEEDS = ((1, 1, 2, 3), (1, 2, 3, 3))
SIZES = (8 * LANE, 4 * LANE, 4 * LANE, 4 * LANE)
STREAMS = len(SIZES)
FIRST = tuple(sum(SIZES[:s]) for s in range(STREAMS))
HALF = sum(SIZES)
PIECE = tuple(size // 8 for size in SIZES)
LAST = tuple(size // 64 for size in SIZES)
LAST_AT = tuple(first // 64 for first in FIRST)
OWN = sum(LAST)
FAR = 4


def places(cc, k):
    at, out = 0, []
    for kind, lo, hi in JOBS[cc]:
        for i in (lo, lo + 1) if kind == "g" else (0,):
            for j in range(max(lo, i), hi):
                out.append((kind, i, j, at))
                at += LANE if kind == "g" else k
    return out


def flip(bit, mask):
    return bit + mask - 2 * bit * mask


def reduce_kernel(dims, slab, panel, g_high, g_low, first, part, got_c, own, got_z, own_t,
                  total, known, sems, *got):
    nz, ny, nx = dims
    k = panel.shape[0]
    got_1, got_2 = got[:STREAMS], got[STREAMS:]

    z = lax.axis_index("rowa")
    b = lax.axis_index("rowb")
    c = lax.rem(b, CORES)
    x = lax.rem(b // CORES, nx)
    y = b // (CORES * nx)

    def device(zz, yy, xx, cc):
        return (zz, (yy * nx + xx) * CORES + cc)

    def ring_pairs(i, n):
        low = lax.rem(i, 2)
        return (lax.rem((i + 1) // 2, 2), i + 1 - 2 * low), (i // 2, n - 1 - i)

    def line_pairs(i, n):
        low = lax.rem(i, 2)
        return (low, i + 1 - 2 * low), (low, lax.rem(i - 1 + 2 * low + n, n))

    z_low, z_at = lax.rem(z, 2), z // 2
    pair_x, pair_y, pair_z = ring_pairs(x, nx), ring_pairs(y, ny), line_pairs(z, nz)
    pair_z2 = tuple((bit, 2 * at + z_low) for bit, at in line_pairs(z_at, nz // 2))

    def pick(pair, family):
        return tuple(a + family * (e - a) for a, e in zip(*pair))

    families = [lax.rem(s + c, 2) for s in range(STREAMS)]
    groups = [
        (
            [pick(pair, f) for pair in (pair_x, pair_y, pair_z)],
            [pick(pair_x, 1 - f), pick(pair_y, 1 - f), pick(pair_z2, f)],
        )
        for f in families
    ]

    def peer(s, step, mask):
        px, py, pz = groups[s][step]
        return device(pz[1] if mask & 4 else z, py[1] if mask & 2 else y, px[1] if mask & 1 else x, c)

    def index(s, step, mask):
        return sum(flip(bit, mask >> i & 1) * (1 << i) for i, (bit, _) in enumerate(groups[s][step]))

    other = device(z, y, x, 1 - c)
    far = [device(lax.rem(z + q * (nz // FAR), nz), y, x, c) for q in range(1, FAR)]

    barrier = pltpu.get_barrier_semaphore()
    everyone = [other] + [peer(s, 0, m) for s in range(2) for m in range(1, 8)]
    everyone += [peer(s, 1, m) for s in range(2) for m in range(4, 8)]
    for device_id in everyone:
        pl.semaphore_signal(barrier, inc=1, device_id=device_id, device_id_type=MESH)

    def tell(level, devices):
        for device_id in devices:
            pl.semaphore_signal(known.at[level], inc=1, device_id=device_id, device_id_type=MESH)

    used, sent, started = [0], [], {}

    def copy(src, dst, at, device_id):
        return pltpu.make_async_remote_copy(
            src_ref=src, dst_ref=dst, send_sem=sems.at[at], recv_sem=sems.at[at + 1],
            device_id=device_id, device_id_type=MESH,
        )

    def start(key, copies, everything):
        at = used[0]
        used[0] += 2
        for src, dst, device_id in copies:
            copy(src, dst, at, device_id).start()
        cp = started[key] = copy(everything, everything, at, other)
        sent.append(cp)

    def drain(count):
        for cp in sent[:count]:
            cp.wait_send()
        del sent[:count]

    def rows(off, count):
        return pl.ds(off if isinstance(off, int) else pl.multiple_of(off, 8), count)

    def work(half, s):
        for cc in range(CORES):
            @pl.when(half == cc)
            def _():
                at = 0
                for number, (kind, lo, hi) in enumerate(JOBS[cc]):
                    mine = (NEEDS[cc][s - 1] if s else 0) <= number < NEEDS[cc][s]
                    if mine and kind == "g":
                        v = dot(slab[:, lo * LANE : (lo + 2) * LANE].T, slab[:, lo * LANE : hi * LANE])
                    elif mine:
                        v = dot(panel[...], slab[:, lo * LANE : hi * LANE])
                    for i in (0, 1) if kind == "g" else (0,):
                        step = LANE if kind == "g" else k
                        for j in range(i, hi - lo):
                            if mine:
                                part[cc, at : at + step, :] = v[i * step : (i + 1) * step, j * LANE : (j + 1) * LANE]
                            at += step

    streams = range(STREAMS)
    off_1 = [FIRST[s] + index(s, 0, 0) * PIECE[s] for s in streams]
    off_2 = [off_1[s] + index(s, 1, 0) * LAST[s] for s in streams]

    for s in streams:
        work(1 - c, s)
        if s == 0:
            pl.semaphore_wait(barrier, len(everyone))
        where = pl.ds(FIRST[s], SIZES[s])
        start(("c", s), [(part.at[1 - c, where], got_c.at[where], other)], got_c.at[where])
    tell(0, [peer(s, 1, 4) for s in range(2)])
    for s in streams:
        work(c, s)
        started["c", s].wait_recv()
        where = pl.ds(FIRST[s], SIZES[s])
        got_c[where, :] = part[c, where, :] + got_c[where, :]
        copies = [
            (got_c.at[rows(FIRST[s] + index(s, 0, m) * PIECE[s], PIECE[s])], got_1[s].at[m - 1], peer(s, 0, m))
            for m in range(7, 0, -1)
        ]
        start((1, s), copies, got_1[s])
    pl.semaphore_wait(known.at[0], 2)
    tell(1, [far[0], far[2]])
    for s in streams:
        started[1, s].wait_recv()
        v = got_c[rows(off_1[s], PIECE[s]), :]
        for m in range(1, 8):
            v = v + got_1[s][m - 1]
        got_c[rows(off_1[s], PIECE[s]), :] = v
        copies = [
            (got_c.at[rows(off_1[s] + index(s, 1, m) * LAST[s], LAST[s])], got_2[s].at[m - 1], peer(s, 1, m))
            for m in range(7, 0, -1)
        ]
        start((2, s), copies, got_2[s])
    me_far = z // (nz // FAR)
    far_at = used[0]
    used[0] += STREAMS * (2 * FAR - 1)

    def far_copy(s, q, slot):
        mine, at = pl.ds(LAST_AT[s], LAST[s]), far_at + s * (2 * FAR - 1)
        return pltpu.make_async_remote_copy(
            src_ref=own.at[mine], dst_ref=got_z.at[slot, mine], send_sem=sems.at[at + q - 1],
            recv_sem=sems.at[at + FAR - 1 + slot], device_id=far[q - 1], device_id_type=MESH,
        )

    before = len(sent)
    pl.semaphore_wait(known.at[1], 2)
    for s in streams:
        started[2, s].wait_recv()
        v = got_c[rows(off_2[s], LAST[s]), :]
        for m in range(1, 8):
            v = v + got_2[s][m - 1]
        own[LAST_AT[s] : LAST_AT[s] + LAST[s], :] = v
        for q in (2, 1, 3):
            far_copy(s, q, me_far).start()
            sent.append(far_copy(s, q, me_far))
        got_z[me_far, LAST_AT[s] : LAST_AT[s] + LAST[s], :] = v
    drain(before)

    for s in streams:
        mine = slice(LAST_AT[s], LAST_AT[s] + LAST[s])
        for q in range(1, FAR):
            far_copy(s, q, lax.rem(me_far + q, FAR)).wait_recv()
        v = got_z[0, mine, :]
        for q in range(1, FAR):
            v = v + got_z[q, mine, :]
        own_t[mine, :] = v
        where = rows(off_2[s], LAST[s])
        src = own_t.at[pl.ds(LAST_AT[s], LAST[s])]
        copies = [(src, total.at[c, where], peer(s, 1, m)) for m in range(7, 0, -1)]
        start((3, s), copies, total.at[c, pl.ds(FIRST[s], 7 * LAST[s])])
        total[c, where, :] = own_t[LAST_AT[s] : LAST_AT[s] + LAST[s], :]
    before = len(sent)
    for s in streams:
        started[3, s].wait_recv()
        where = total.at[c, rows(off_1[s], PIECE[s])]
        for part_at, masks in enumerate(((3, 2, 1), (7, 6, 5, 4))):
            copies = [(where, where, peer(s, 0, m)) for m in masks]
            start((4, s, part_at), copies, total.at[c, pl.ds(FIRST[s], len(masks) * PIECE[s])])
    drain(before)
    for s in streams:
        for part_at in range(2):
            started[4, s, part_at].wait_recv()
            begin = FIRST[s] + flip(z_low, part_at) * 4 * PIECE[s]
            where = total.at[c, rows(begin, 4 * PIECE[s])]
            start((5, s, part_at), [(where, where, other)], where)

    def whole(half, s):
        for cc in range(CORES):
            @pl.when(half == cc)
            def _():
                for kind, i, j, at in places(cc, k):
                    if not FIRST[s] <= at < FIRST[s] + SIZES[s]:
                        continue
                    if kind == "p":
                        first[:, j * LANE : (j + 1) * LANE] = total[cc, at : at + k, :]
                        continue
                    v = total[cc, at : at + LANE, :]
                    for a, e, w in ((i, j, v), (j, i, v.T))[: 2 if j > i else 1]:
                        high, low = split(w)
                        g_high[a * LANE : (a + 1) * LANE, e * LANE : (e + 1) * LANE] = high
                        g_low[a * LANE : (a + 1) * LANE, e * LANE : (e + 1) * LANE] = low

    for s in streams:
        whole(c, s)
    drain(len(sent) - 2 * STREAMS)
    for s in streams:
        for part_at in range(2):
            started[5, s, part_at].wait_recv()
        whole(1 - c, s)
    drain(len(sent))


def passes_kernel(scale, slab, g_high, g_low, first, basis_ref, factor_ref, w_high, w_low, w_both, p_pad):
    k, d = first.shape
    w_high[0:k, :] = jnp.zeros((k, d), BF16)
    w_low[0:k, :] = jnp.zeros((k, d), BF16)
    p_pad[k : 2 * k, :] = jnp.zeros((k, d), BF16)
    current = first[...]
    row = lax.broadcasted_iota(jnp.int32, (k, 2 * k), 0)
    col = lax.broadcasted_iota(jnp.int32, (k, 2 * k), 1)
    eye = jnp.where(col == row + k, 1.0, 0.0)
    for step in range(ITERS):
        pb = current.astype(BF16)
        p_pad[0:k, :] = pb
        wh, wl = split(dot(pb, g_high[...]) + dot(pb, g_low[...]))
        if step == ITERS - 1:
            rows = slab.shape[0]
            ih, il = split(dot_t(pb, slab[...]))
        w_both[0:k, :] = wh
        w_both[k : 2 * k, :] = wl
        gram = dot_t(w_both[...], p_pad[...])
        m = factor_rows(gram[0:k, :] + gram[k : 2 * k, :] + eye, k)
        mh, ml = split(m)
        if step < ITERS - 1:
            w_high[k : 2 * k, :] = wh
            w_low[k : 2 * k, :] = wl
            both = dot(jnp.concatenate([mh, ml], axis=0), w_high[...])
            current = both[0:k, :] + (dot(mh, w_low[...]) + both[k : 2 * k, :])
        else:
            w_high[k : 2 * k, 0:rows] = ih
            w_low[k : 2 * k, 0:rows] = il
            ih, il = w_high[:, 0:rows], w_low[:, 0:rows]
            basis_ref[...] = (dot(mh, ih) + (dot(mh, il) + dot(ml, ih))) * scale
            factor_ref[...] = jnp.where(col >= row, m, 0.0)[:, 0:k] * (1.0 / scale)


def body(sizes, slab, panel):
    nz, ny, nx = sizes
    rows, d = slab.shape
    k = panel.shape[0]
    scale = math.sqrt(rows * nz * ny * nx * CORES)
    n_sems = STREAMS * (16 + 2 * FAR - 1)
    params = functools.partial(pltpu.CompilerParams, vmem_limit_bytes=36 * 1024 * 1024)
    vmem = pl.BlockSpec(memory_space=pltpu.VMEM)

    g_high, g_low, first = pl.pallas_call(
        functools.partial(reduce_kernel, (nz, ny, nx)),
        out_shape=(
            jax.ShapeDtypeStruct((d, d), BF16), jax.ShapeDtypeStruct((d, d), BF16), jax.ShapeDtypeStruct((k, d), F32)
        ),
        in_specs=[vmem] * 2,
        out_specs=(vmem,) * 3,
        scratch_shapes=[
            pltpu.VMEM((CORES, HALF, LANE), F32),
            pltpu.VMEM((HALF, LANE), F32),
            pltpu.VMEM((OWN, LANE), F32),
            pltpu.VMEM((FAR, OWN, LANE), F32),
            pltpu.VMEM((OWN, LANE), F32),
            pltpu.VMEM((CORES, HALF, LANE), F32),
            pltpu.SemaphoreType.REGULAR((2,)),
            pltpu.SemaphoreType.DMA((n_sems,)),
            *[pltpu.VMEM((7, size, LANE), F32) for size in PIECE + LAST],
        ],
        compiler_params=params(collective_id=0, has_side_effects=True),
        cost_estimate=pl.CostEstimate(flops=10**9, bytes_accessed=10**7, transcendentals=0),
    )(slab, panel)
    return pl.pallas_call(
        functools.partial(passes_kernel, scale),
        out_shape=(jax.ShapeDtypeStruct((k, rows), F32), jax.ShapeDtypeStruct((k, k), F32)),
        in_specs=[vmem] * 4,
        out_specs=(vmem,) * 2,
        scratch_shapes=[
            pltpu.VMEM((2 * k, d), BF16),
            pltpu.VMEM((2 * k, d), BF16),
            pltpu.VMEM((2 * k, d), BF16),
            pltpu.VMEM((2 * k, d), BF16),
        ],
        compiler_params=params(),
        cost_estimate=pl.CostEstimate(flops=2 * 10**9, bytes_accessed=3 * 10**6, transcendentals=0),
    )(slab, g_high, g_low, first)


def solution(mesh):
    nz = mesh.shape["rowa"]
    side = math.isqrt(mesh.shape["rowb"] // CORES)
    in_specs = (P(("rowa", "rowb"), None), P(None, ("rowa", "rowb")))
    out_specs = (P(None, ("rowa", "rowb")), P())
    return jax.shard_map(
        functools.partial(body, (nz, side, side)),
        mesh=mesh, in_specs=in_specs, out_specs=out_specs, check_vma=False,
    )
```

```python
import functools
import math

import jax
import jax.numpy as jnp
from jax import lax
from jax.experimental import pallas as pl
from jax.experimental.pallas import tpu as pltpu
from jax.sharding import PartitionSpec as P

ITERS = 3
MESH = pl.DeviceIdType.MESH
F32 = jnp.float32
BF16 = jnp.bfloat16
LANE = 128
CORES = 2
PANEL = 8


def dot(a, b):
    return jnp.dot(a, b, preferred_element_type=F32)


def dot_t(a, b):
    return lax.dot_general(a, b, (((1,), (1,)), ((), ())), preferred_element_type=F32)


def split(v):
    high = v.astype(BF16)
    return high, (v - high.astype(F32)).astype(BF16)


def factor_rows(m, k):
    groups = [m[8 * i : 8 * i + 8, :] for i in range(k // 8)]
    full = groups[0].shape
    done = [[None] * 8 for _ in groups]
    for first in range(0, k, PANEL):
        g, s = divmod(first, 8)
        size = range(PANEL)
        rows = [jnp.broadcast_to(groups[g][s + q : s + q + 1, :], full) for q in size]
        cols = [
            {i: jnp.broadcast_to(groups[i][:, first + q : first + q + 1], full) for i in range(g + 1, len(groups))}
            for q in size
        ]
        piv = [[jnp.broadcast_to(rows[q][:, first + r : first + r + 1], full) for r in size] for q in size]
        inv = []
        for q in size:
            inv.append(pl.reciprocal(piv[q][q]))
            for r in range(q + 1, PANEL):
                t = piv[q][r] * inv[q]
                rows[r] = rows[r] - t * rows[q]
                for i in cols[r]:
                    cols[r][i] = cols[r][i] - t * cols[q][i]
                for w in range(r, PANEL):
                    piv[r][w] = piv[r][w] - t * piv[q][w]
            done[g][s + q] = rows[q] * lax.rsqrt(piv[q][q])
        scaled = [rows[q] * inv[q] for q in size]
        for i in range(g + 1, len(groups)):
            for q in size:
                groups[i] = groups[i] - cols[q][i] * scaled[q]
    sub = lax.broadcasted_iota(jnp.int32, full, 0)
    out = []
    for rows in done:
        v = rows[0]
        for q in range(1, 8):
            v = jnp.where(sub == q, rows[q], v)
        out.append(v)
    return jnp.concatenate(out, axis=0)


JOBS = ((("g", 0, 8), ("g", 6, 8), ("p", 0, 4)), (("g", 2, 8), ("p", 4, 8), ("g", 4, 8)))
NEEDS = ((1, 1, 1, 2, 3), (1, 1, 2, 3, 3))
SIZES = (4 * LANE,) * 5
STREAMS = len(SIZES)
FIRST = tuple(sum(SIZES[:s]) for s in range(STREAMS))
HALF = sum(SIZES)
PIECE = tuple(size // 8 for size in SIZES)
LAST = tuple(size // 64 for size in SIZES)
LAST_AT = tuple(first // 64 for first in FIRST)
OWN = sum(LAST)
FAR = 4


def places(cc, k):
    at, out = 0, []
    for kind, lo, hi in JOBS[cc]:
        for i in (lo, lo + 1) if kind == "g" else (0,):
            for j in range(max(lo, i), hi):
                out.append((kind, i, j, at))
                at += LANE if kind == "g" else k
    return out


def flip(bit, mask):
    return bit + mask - 2 * bit * mask


def reduce_kernel(dims, slab, panel, g_high, g_low, first, part, got_c, own, got_z, own_t,
                  total, known, sems, *got):
    nz, ny, nx = dims
    k = panel.shape[0]
    got_1, got_2 = got[:STREAMS], got[STREAMS:]

    z = lax.axis_index("rowa")
    b = lax.axis_index("rowb")
    c = lax.rem(b, CORES)
    x = lax.rem(b // CORES, nx)
    y = b // (CORES * nx)

    def device(zz, yy, xx, cc):
        return (zz, (yy * nx + xx) * CORES + cc)

    def ring_pairs(i, n):
        low = lax.rem(i, 2)
        return (lax.rem((i + 1) // 2, 2), i + 1 - 2 * low), (i // 2, n - 1 - i)

    def line_pairs(i, n):
        low = lax.rem(i, 2)
        return (low, i + 1 - 2 * low), (low, lax.rem(i - 1 + 2 * low + n, n))

    z_low, z_at = lax.rem(z, 2), z // 2
    pair_x, pair_y, pair_z = ring_pairs(x, nx), ring_pairs(y, ny), line_pairs(z, nz)
    pair_z2 = tuple((bit, 2 * at + z_low) for bit, at in line_pairs(z_at, nz // 2))

    def pick(pair, family):
        return tuple(a + family * (e - a) for a, e in zip(*pair))

    families = [lax.rem(s + c, 2) for s in range(STREAMS)]
    groups = [
        (
            [pick(pair, f) for pair in (pair_x, pair_y, pair_z)],
            [pick(pair_x, 1 - f), pick(pair_y, 1 - f), pick(pair_z2, f)],
        )
        for f in families
    ]

    def peer(s, step, mask):
        px, py, pz = groups[s][step]
        return device(pz[1] if mask & 4 else z, py[1] if mask & 2 else y, px[1] if mask & 1 else x, c)

    def index(s, step, mask):
        return sum(flip(bit, mask >> i & 1) * (1 << i) for i, (bit, _) in enumerate(groups[s][step]))

    other = device(z, y, x, 1 - c)
    far = [device(lax.rem(z + q * (nz // FAR), nz), y, x, c) for q in range(1, FAR)]

    barrier = pltpu.get_barrier_semaphore()
    everyone = [other] + [peer(s, 0, m) for s in range(2) for m in range(1, 8)]
    everyone += [peer(s, 1, m) for s in range(2) for m in range(4, 8)]
    for device_id in everyone:
        pl.semaphore_signal(barrier, inc=1, device_id=device_id, device_id_type=MESH)

    def tell(level, devices):
        for device_id in devices:
            pl.semaphore_signal(known.at[level], inc=1, device_id=device_id, device_id_type=MESH)

    used, sent, started = [0], [], {}

    def copy(src, dst, at, device_id):
        return pltpu.make_async_remote_copy(
            src_ref=src, dst_ref=dst, send_sem=sems.at[at], recv_sem=sems.at[at + 1],
            device_id=device_id, device_id_type=MESH,
        )

    def start(key, copies, everything):
        at = used[0]
        used[0] += 2
        for src, dst, device_id in copies:
            copy(src, dst, at, device_id).start()
        cp = started[key] = copy(everything, everything, at, other)
        sent.append(cp)

    def drain(count):
        for cp in sent[:count]:
            cp.wait_send()
        del sent[:count]

    def rows(off, count):
        return pl.ds(off if isinstance(off, int) else pl.multiple_of(off, 8), count)

    def work(half, s):
        for cc in range(CORES):
            @pl.when(half == cc)
            def _():
                at = 0
                for number, (kind, lo, hi) in enumerate(JOBS[cc]):
                    mine = (NEEDS[cc][s - 1] if s else 0) <= number < NEEDS[cc][s]
                    if mine and kind == "g":
                        v = dot(slab[:, lo * LANE : (lo + 2) * LANE].T, slab[:, lo * LANE : hi * LANE])
                    elif mine:
                        v = dot(panel[...], slab[:, lo * LANE : hi * LANE])
                    for i in (0, 1) if kind == "g" else (0,):
                        step = LANE if kind == "g" else k
                        for j in range(i, hi - lo):
                            if mine:
                                part[cc, at : at + step, :] = v[i * step : (i + 1) * step, j * LANE : (j + 1) * LANE]
                            at += step

    streams = range(STREAMS)
    off_1 = [FIRST[s] + index(s, 0, 0) * PIECE[s] for s in streams]
    off_2 = [off_1[s] + index(s, 1, 0) * LAST[s] for s in streams]

    for s in streams:
        work(1 - c, s)
        if s == 0:
            pl.semaphore_wait(barrier, len(everyone))
        where = pl.ds(FIRST[s], SIZES[s])
        start(("c", s), [(part.at[1 - c, where], got_c.at[where], other)], got_c.at[where])
    tell(0, [peer(s, 1, 4) for s in range(2)])
    for s in streams:
        work(c, s)
        started["c", s].wait_recv()
        where = pl.ds(FIRST[s], SIZES[s])
        got_c[where, :] = part[c, where, :] + got_c[where, :]
        copies = [
            (got_c.at[rows(FIRST[s] + index(s, 0, m) * PIECE[s], PIECE[s])], got_1[s].at[m - 1], peer(s, 0, m))
            for m in range(7, 0, -1)
        ]
        start((1, s), copies, got_1[s])
    pl.semaphore_wait(known.at[0], 2)
    tell(1, [far[0], far[2]])
    for s in streams:
        started[1, s].wait_recv()
        v = got_c[rows(off_1[s], PIECE[s]), :]
        for m in range(1, 8):
            v = v + got_1[s][m - 1]
        got_c[rows(off_1[s], PIECE[s]), :] = v
        copies = [
            (got_c.at[rows(off_1[s] + index(s, 1, m) * LAST[s], LAST[s])], got_2[s].at[m - 1], peer(s, 1, m))
            for m in range(7, 0, -1)
        ]
        start((2, s), copies, got_2[s])
    me_far = z // (nz // FAR)
    far_at = used[0]
    used[0] += STREAMS * (2 * FAR - 1)

    def far_copy(s, q, slot):
        mine, at = pl.ds(LAST_AT[s], LAST[s]), far_at + s * (2 * FAR - 1)
        return pltpu.make_async_remote_copy(
            src_ref=own.at[mine], dst_ref=got_z.at[slot, mine], send_sem=sems.at[at + q - 1],
            recv_sem=sems.at[at + FAR - 1 + slot], device_id=far[q - 1], device_id_type=MESH,
        )

    before = len(sent)
    pl.semaphore_wait(known.at[1], 2)
    for s in streams:
        started[2, s].wait_recv()
        v = got_c[rows(off_2[s], LAST[s]), :]
        for m in range(1, 8):
            v = v + got_2[s][m - 1]
        own[LAST_AT[s] : LAST_AT[s] + LAST[s], :] = v
        for q in (2, 1, 3):
            far_copy(s, q, me_far).start()
            sent.append(far_copy(s, q, me_far))
        got_z[me_far, LAST_AT[s] : LAST_AT[s] + LAST[s], :] = v
    drain(before)

    for s in streams:
        mine = slice(LAST_AT[s], LAST_AT[s] + LAST[s])
        for q in range(1, FAR):
            far_copy(s, q, lax.rem(me_far + q, FAR)).wait_recv()
        v = got_z[0, mine, :]
        for q in range(1, FAR):
            v = v + got_z[q, mine, :]
        own_t[mine, :] = v
        where = rows(off_2[s], LAST[s])
        src = own_t.at[pl.ds(LAST_AT[s], LAST[s])]
        copies = [(src, total.at[c, where], peer(s, 1, m)) for m in range(7, 0, -1)]
        start((3, s), copies, total.at[c, pl.ds(FIRST[s], 7 * LAST[s])])
        total[c, where, :] = own_t[LAST_AT[s] : LAST_AT[s] + LAST[s], :]
    before = len(sent)
    for s in streams:
        started[3, s].wait_recv()
        where = total.at[c, rows(off_1[s], PIECE[s])]
        for part_at, masks in enumerate(((3, 2, 1), (7, 6, 5, 4))):
            copies = [(where, where, peer(s, 0, m)) for m in masks]
            start((4, s, part_at), copies, total.at[c, pl.ds(FIRST[s], len(masks) * PIECE[s])])
    drain(before)
    for s in streams:
        for part_at in range(2):
            started[4, s, part_at].wait_recv()
            begin = FIRST[s] + flip(z_low, part_at) * 4 * PIECE[s]
            where = total.at[c, rows(begin, 4 * PIECE[s])]
            start((5, s, part_at), [(where, where, other)], where)

    def whole(half, s):
        for cc in range(CORES):
            @pl.when(half == cc)
            def _():
                for kind, i, j, at in places(cc, k):
                    if not FIRST[s] <= at < FIRST[s] + SIZES[s]:
                        continue
                    if kind == "p":
                        first[:, j * LANE : (j + 1) * LANE] = total[cc, at : at + k, :]
                        continue
                    v = total[cc, at : at + LANE, :]
                    for a, e, w in ((i, j, v), (j, i, v.T))[: 2 if j > i else 1]:
                        high, low = split(w)
                        g_high[a * LANE : (a + 1) * LANE, e * LANE : (e + 1) * LANE] = high
                        g_low[a * LANE : (a + 1) * LANE, e * LANE : (e + 1) * LANE] = low

    for s in streams:
        whole(c, s)
    drain(len(sent) - 2 * STREAMS)
    for s in streams:
        for part_at in range(2):
            started[5, s, part_at].wait_recv()
        whole(1 - c, s)
    drain(len(sent))


def passes_kernel(scale, slab, g_high, g_low, first, basis_ref, factor_ref, w_high, w_low, w_both, p_pad):
    k, d = first.shape
    w_high[0:k, :] = jnp.zeros((k, d), BF16)
    w_low[0:k, :] = jnp.zeros((k, d), BF16)
    p_pad[k : 2 * k, :] = jnp.zeros((k, d), BF16)
    current = first[...]
    row = lax.broadcasted_iota(jnp.int32, (k, 2 * k), 0)
    col = lax.broadcasted_iota(jnp.int32, (k, 2 * k), 1)
    eye = jnp.where(col == row + k, 1.0, 0.0)
    for step in range(ITERS):
        pb = current.astype(BF16)
        p_pad[0:k, :] = pb
        wh, wl = split(dot(pb, g_high[...]) + dot(pb, g_low[...]))
        if step == ITERS - 1:
            rows = slab.shape[0]
            ih, il = split(dot_t(pb, slab[...]))
        w_both[0:k, :] = wh
        w_both[k : 2 * k, :] = wl
        gram = dot_t(w_both[...], p_pad[...])
        m = factor_rows(gram[0:k, :] + gram[k : 2 * k, :] + eye, k)
        mh, ml = split(m)
        if step < ITERS - 1:
            w_high[k : 2 * k, :] = wh
            w_low[k : 2 * k, :] = wl
            both = dot(jnp.concatenate([mh, ml], axis=0), w_high[...])
            current = both[0:k, :] + (dot(mh, w_low[...]) + both[k : 2 * k, :])
        else:
            w_high[k : 2 * k, 0:rows] = ih
            w_low[k : 2 * k, 0:rows] = il
            ih, il = w_high[:, 0:rows], w_low[:, 0:rows]
            basis_ref[...] = (dot(mh, ih) + (dot(mh, il) + dot(ml, ih))) * scale
            factor_ref[...] = jnp.where(col >= row, m, 0.0)[:, 0:k] * (1.0 / scale)


def body(sizes, slab, panel):
    nz, ny, nx = sizes
    rows, d = slab.shape
    k = panel.shape[0]
    scale = math.sqrt(rows * nz * ny * nx * CORES)
    n_sems = STREAMS * (16 + 2 * FAR - 1)
    params = functools.partial(pltpu.CompilerParams, vmem_limit_bytes=36 * 1024 * 1024)
    vmem = pl.BlockSpec(memory_space=pltpu.VMEM)

    g_high, g_low, first = pl.pallas_call(
        functools.partial(reduce_kernel, (nz, ny, nx)),
        out_shape=(
            jax.ShapeDtypeStruct((d, d), BF16), jax.ShapeDtypeStruct((d, d), BF16), jax.ShapeDtypeStruct((k, d), F32)
        ),
        in_specs=[vmem] * 2,
        out_specs=(vmem,) * 3,
        scratch_shapes=[
            pltpu.VMEM((CORES, HALF, LANE), F32),
            pltpu.VMEM((HALF, LANE), F32),
            pltpu.VMEM((OWN, LANE), F32),
            pltpu.VMEM((FAR, OWN, LANE), F32),
            pltpu.VMEM((OWN, LANE), F32),
            pltpu.VMEM((CORES, HALF, LANE), F32),
            pltpu.SemaphoreType.REGULAR((2,)),
            pltpu.SemaphoreType.DMA((n_sems,)),
            *[pltpu.VMEM((7, size, LANE), F32) for size in PIECE + LAST],
        ],
        compiler_params=params(collective_id=0, has_side_effects=True),
        cost_estimate=pl.CostEstimate(flops=10**9, bytes_accessed=10**7, transcendentals=0),
    )(slab, panel)
    return pl.pallas_call(
        functools.partial(passes_kernel, scale),
        out_shape=(jax.ShapeDtypeStruct((k, rows), F32), jax.ShapeDtypeStruct((k, k), F32)),
        in_specs=[vmem] * 4,
        out_specs=(vmem,) * 2,
        scratch_shapes=[
            pltpu.VMEM((2 * k, d), BF16),
            pltpu.VMEM((2 * k, d), BF16),
            pltpu.VMEM((2 * k, d), BF16),
            pltpu.VMEM((2 * k, d), BF16),
        ],
        compiler_params=params(),
        cost_estimate=pl.CostEstimate(flops=2 * 10**9, bytes_accessed=3 * 10**6, transcendentals=0),
    )(slab, g_high, g_low, first)


def solution(mesh):
    nz = mesh.shape["rowa"]
    side = math.isqrt(mesh.shape["rowb"] // CORES)
    in_specs = (P(("rowa", "rowb"), None), P(None, ("rowa", "rowb")))
    out_specs = (P(None, ("rowa", "rowb")), P())
    return jax.shard_map(
        functools.partial(body, (nz, side, side)),
        mesh=mesh, in_specs=in_specs, out_specs=out_specs, check_vma=False,
    )
```
